32 devices in a mesh: section: 2 (over x), dp: 8 (over z, y), tensor: 2 (over core).
Axes of the slice: x: 2, y: 2, z: 4, core: 2. Of those that a mesh axis runs over, the one named last changes fastest.
Arguments:
- x_in: bfloat16 [2, 2048, 2048], P(None, 'dp'), may hold values from -6 to 6
- cotangent: bfloat16 [2, 2048, 2048], P(None, 'dp'), may hold values from -6 to 6
- layout: int32 [2, 2048], P(None, 'dp'), may hold values from 0 to 2, as said below
- w_qkv: bfloat16 [2, 2048, 3, 2048], P('section', 'dp', None, 'tensor'), may hold values from -0.125 to 0.125
- b_qv: float32 [2, 2, 2048], P('section', None, 'tensor'), may hold values from -3 to 3
- w_out: bfloat16 [2, 2048, 2048], P('section', 'dp', 'tensor'), may hold values from -0.5 to 0.5
- w_fc1: bfloat16 [2, 2048, 8192], P('section', 'dp', 'tensor'), may hold values from -0.125 to 0.125
- b_fc1: float32 [2, 8192], P('section', 'tensor'), may hold values from -3 to 3
- w_fc2: bfloat16 [2, 2048, 8192], P('section', 'dp', 'tensor'), may hold values from -0.0625 to 0.0625
- gains: float32 [2, 2, 2048], P('section'), may hold values from 0.25 to 1.75
- biases: float32 [2, 4, 2048], P('section'), may hold values from -2 to 2
Outputs:
- section_outputs: bfloat16 [2, 2, 2048, 2048], P('section', None, 'dp')
- input_grads: bfloat16 [2, 2, 2048, 2048], P('section', None, 'dp')
- grad_w_qkv: float32 [2, 2048, 3, 2048], P('section', 'dp', None, 'tensor')
- grad_b_qv: float32 [2, 2, 2048], P('section', None, 'tensor')
- grad_w_out: float32 [2, 2048, 2048], P('section', 'dp', 'tensor')
- grad_w_fc1: float32 [2, 2048, 8192], P('section', 'dp', 'tensor')
- grad_b_fc1: float32 [2, 8192], P('section', 'tensor')
- grad_w_fc2: float32 [2, 2048, 8192], P('section', 'dp', 'tensor')
- grad_gains: float32 [2, 2, 2048], P('section')
- grad_biases: float32 [2, 4, 2048], P('section')
The draws below stay inside these ranges and needn't reach their ends.
Inputs may be any that keep to these rules, and one draw needn't show every extreme that they name: `layout`: in each group of 256 tokens the segment numbers never fall: a prompt of segment 0 with 64 to 128 tokens, then continuations 1 to 2 in order, each non-empty, of nearly equal lengths.
All inputs are finite; a program needn't handle non-finite values.
Results may differ from the reference program's by a relative error of at most 0.018.
Values may be sent and summed in bfloat16 or wider, within the bound.
A program may use at most 384 MiB of HBM per device.

```python
import jax
import jax.numpy as jnp
from jax import lax

D = 2048
HEADS = 32
HEAD_DIM = 64
FF = 8192
GROUP = 256
NCONT = 2
MB = 2
TOKENS = 2048
N_SECTION = 2


def draw_layout(key, part):
    key = jax.random.fold_in(key, 7)
    group_count = MB * (TOKENS // GROUP)
    prompt_len = jax.random.randint(key, (group_count, 1), GROUP // 4, GROUP // 2 + 1).astype(jnp.int32)
    places = jnp.arange(GROUP, dtype=jnp.int32)[None, :]
    remaining = GROUP - prompt_len
    segment = jnp.where(places < prompt_len, 0, 1 + (places - prompt_len) * NCONT // remaining)
    return segment.astype(jnp.int32).reshape(MB, TOKENS)


def levels(stream_key, dims, pieces, low, largest):
    gain, own = 1.0, jax.random.fold_in(stream_key, 6)
    for dim, shards_of in pieces:
        steps = jnp.exp(jax.random.uniform(jax.random.fold_in(own, dim), (shards_of,), jnp.float32, low / len(pieces), largest / len(pieces)))
        gain = gain * jnp.repeat(steps, dims[dim] // shards_of).reshape([-1 if axis == dim else 1 for axis in range(len(dims))])
    return gain


def noise(key, extent, scale, reach, split=(), kind=jnp.bfloat16):
    values = jax.random.normal(key, extent, jnp.float32) * scale
    if len(split) > 0:
        values = levels(key, extent, split, -0.22, 0.18) * values
    return jnp.clip(values, min=-reach, max=reach).astype(kind)


def setup_inputs(seed: int = 0) -> dict:
    key_list = jax.random.split(jax.random.key(seed), 12)
    return {
        "x_in": noise(key_list[0], (MB, TOKENS, D), 1.0, 6.0, ((1, 8),)),
        "cotangent": noise(key_list[1], (MB, TOKENS, D), 1.0, 6.0, ((1, 8),)),
        "layout": draw_layout(jax.random.fold_in(key_list[11], 71), 0),
        "w_qkv": noise(key_list[3], (N_SECTION, D, 3, D), D ** -0.5, 0.125, ((0, 2), (1, 8), (3, 2))),
        "b_qv": noise(key_list[4], (N_SECTION, 2, D), 0.5, 3.0, ((0, 2), (2, 2)), jnp.float32),
        "w_out": noise(key_list[5], (N_SECTION, D, D), (D // 16) ** -0.5, 0.5, ((0, 2), (1, 8), (2, 2))),
        "w_fc1": noise(key_list[6], (N_SECTION, D, FF), D ** -0.5, 0.125, ((0, 2), (1, 8), (2, 2))),
        "b_fc1": noise(key_list[7], (N_SECTION, FF), 0.5, 3.0, ((0, 2), (1, 2)), jnp.float32),
        "w_fc2": noise(key_list[8], (N_SECTION, D, FF), FF ** -0.5, 0.0625, ((0, 2), (1, 8), (2, 2))),
        "gains": jnp.clip(1.0 + 0.15 * jax.random.normal(key_list[9], (N_SECTION, 2, D), jnp.float32), 0.25, 1.75),
        "biases": noise(key_list[10], (N_SECTION, 4, D), 0.3, 2.0, ((0, 2),), jnp.float32),
    }


@jax.custom_vjp
def low(v):
    return lax.optimization_barrier(v.astype(jnp.bfloat16)).astype(jnp.float32)

@jax.custom_vjp
def low_back(v):
    return v

def low_keep(v):
    return (low(v), None)

def low_pass(kept, grad):
    return (grad,)

def back_keep(v):
    return (v, None)

def back_low(kept, grad):
    return (low(grad),)
low.defvjp(low_keep, low_pass)
low_back.defvjp(back_keep, back_low)
highest = lax.Precision.HIGHEST
epsilon = 1e-05

def layer_norm(inputs, gain_vec, shift_vec):
    centred = inputs - lax.optimization_barrier(jnp.mean(inputs, axis=-1, keepdims=True))
    spread = lax.optimization_barrier(jnp.mean(centred * centred, axis=-1, keepdims=True))
    return centred * lax.rsqrt(spread + epsilon) * gain_vec + shift_vec

def exact_gelu(values):
    return jax.nn.gelu(values, approximate=False)

def geometry(segment):
    length = segment.shape[0]
    places = jnp.arange(length, dtype=jnp.int32)
    same_seg = segment[:, None] == segment[None, :]
    starts = lax.optimization_barrier(jnp.min(jnp.where(same_seg, places[None, :], length), axis=1)).astype(jnp.int32)
    prompt_len = jnp.sum((segment == 0).astype(jnp.int32))
    position = jnp.where(segment == 0, places, prompt_len + places - starts)
    allowed = (position[None, :] <= position[:, None]) & ((segment[None, :] == 0) | same_seg)
    offset = (position[:, None] - position[None, :]).astype(jnp.float32)
    return (offset, allowed)

def layer(params, inputs, segment):
    w_attn, bias_qv, w_proj, w_up, bias_up, w_down, gain_rows, shift_rows = params
    row_count = inputs.shape[0]
    score_scale = float(HEAD_DIM) ** (-0.5)
    normed = low(layer_norm(inputs, gain_rows[0], shift_rows[0]))
    projected = jnp.einsum('gd,dcf->gcf', normed, w_attn, precision=highest)
    queries = low(low_back(projected[:, 0] + bias_qv[0])).reshape(row_count, HEADS, HEAD_DIM)
    key_rows = low(low_back(projected[:, 1])).reshape(row_count, HEADS, HEAD_DIM)
    value_rows = low(low_back(projected[:, 2] + bias_qv[1])).reshape(row_count, HEADS, HEAD_DIM)
    offset, allowed = geometry(segment)
    slopes = jnp.exp2(-8.0 * jnp.arange(1, HEADS + 1).astype(jnp.float32) / HEADS)
    scores = jnp.einsum('qhd,khd->hqk', queries, key_rows, precision=highest) * score_scale
    scores = scores - slopes[:, None, None] * offset[None]
    scores = low_back(jnp.where(allowed[None], scores, -1000000000.0))
    probs = low(jax.nn.softmax(scores, axis=-1))
    mixed = jnp.einsum('hqk,khd->qhd', probs, value_rows, precision=highest).reshape(row_count, HEADS * HEAD_DIM)
    mixed = low(low_back(mixed))
    branch = jnp.dot(mixed, w_proj.T, precision=highest)
    hidden = inputs + low_back(branch) + shift_rows[2]
    normed_two = low(layer_norm(hidden, gain_rows[1], shift_rows[1]))
    upward = low_back(jnp.dot(normed_two, w_up, precision=highest) + bias_up)
    activated = low(exact_gelu(upward))
    down_sum = jnp.dot(activated, w_down.T, precision=highest)
    return hidden + low_back(down_sum) + shift_rows[3]

def reference(x_in, cotangent, layout, w_qkv, b_qv, w_out, w_fc1, b_fc1, w_fc2, gains, biases):
    group_count = TOKENS // GROUP
    total_groups = MB * group_count
    inputs = x_in.astype(jnp.float32).reshape(total_groups, GROUP, D)
    cotans = cotangent.astype(jnp.float32).reshape(total_groups, GROUP, D)
    segments = layout.reshape(total_groups, GROUP)
    weight_list = (w_qkv, b_qv, w_out, w_fc1, b_fc1, w_fc2, gains, biases)
    sections = tuple((tuple((weight_arr[section_num].astype(jnp.float32) for weight_arr in weight_list)) for section_num in range(N_SECTION)))
    zero_grads = jax.tree.map(jnp.zeros_like, sections)

    def one_group(carry, item):
        group_in, group_cot, segment = item
        outputs_here = []
        pullbacks = []
        current = group_in
        for section_num in range(N_SECTION):
            result, pullback = jax.vjp(lambda params, values: layer(params, values, segment), sections[section_num], current)
            outputs_here.append(result.astype(jnp.bfloat16))
            pullbacks.append(pullback)
            current = result.astype(jnp.bfloat16).astype(jnp.float32)
        gradient = group_cot
        grads_here = [None] * N_SECTION
        new_carry = list(carry)
        for section_num in reversed(range(N_SECTION)):
            grad_params, grad_input = pullbacks[section_num](gradient)
            new_carry[section_num] = jax.tree.map(jnp.add, carry[section_num], grad_params)
            grads_here[section_num] = grad_input.astype(jnp.bfloat16)
            gradient = grads_here[section_num].astype(jnp.float32)
        return (tuple(new_carry), (jnp.stack(outputs_here), jnp.stack(grads_here)))
    final_grads, (outputs_all, grads_all) = lax.scan(one_group, zero_grads, (inputs, cotans, segments))

    def arrange(stacked):
        shaped = stacked.reshape(MB, group_count, N_SECTION, GROUP, D)
        return jnp.transpose(shaped, (2, 0, 1, 3, 4)).reshape(N_SECTION, MB, TOKENS, D)

    def gather_grad(position_in):
        return jnp.stack([final_grads[section_num][position_in] for section_num in range(N_SECTION)])
    return (arrange(outputs_all), arrange(grads_all), gather_grad(0), gather_grad(1), gather_grad(2), gather_grad(3), gather_grad(4), gather_grad(5), gather_grad(6), gather_grad(7))
```

```python
import jax
import jax.numpy as jnp
from jax import lax
from jax.sharding import Mesh, PartitionSpec as P

HEADS = 32
HEAD_DIM = 64
GROUP = 256
EPS = 1e-05
BF = jnp.bfloat16
F32 = jnp.float32
DP = ("zh", "zl", "y")


def dot(a, b):
    return jnp.dot(a, b, preferred_element_type=F32)


def dot_t(a, b):
    return lax.dot_general(a, b, (((1,), (1,)), ((), ())), preferred_element_type=F32)


def row_dot(a, b):
    return lax.dot_general(a, b, (((0,), (0,)), ((), ())), preferred_element_type=F32)


def swap(v, axis, offset=1):
    n = lax.axis_size(axis)
    return lax.ppermute(v, axis, [(i, i ^ offset) for i in range(n)])


def pick(v, index, dim):
    return lax.dynamic_index_in_dim(v, index, dim, keepdims=False)


def in_order(mine, other, index, dim):
    first = jnp.where(index == 0, mine, other)
    second = jnp.where(index == 0, other, mine)
    return jnp.stack([first, second], axis=dim)


def normalize(v):
    centred = v - jnp.mean(v, axis=-1, keepdims=True)
    scale = lax.rsqrt(jnp.mean(centred * centred, axis=-1, keepdims=True) + EPS)
    return centred * scale, scale


def gelu_parts(u):
    cdf = 0.5 * (1.0 + lax.erf(u * (0.5**0.5)))
    pdf = jnp.exp(-0.5 * u * u) * 0.3989422804014327
    return u * cdf, cdf + u * pdf


def geometry(segment):
    length = segment.shape[0]
    places = jnp.arange(length, dtype=jnp.int32)
    same_seg = segment[:, None] == segment[None, :]
    starts = jnp.min(jnp.where(same_seg, places[None, :], length), axis=1)
    prompt_len = jnp.sum((segment == 0).astype(jnp.int32))
    position = jnp.where(segment == 0, places, prompt_len + places - starts)
    allowed = (position[None, :] <= position[:, None]) & ((segment[None, :] == 0) | same_seg)
    offset = (position[:, None] - position[None, :]).astype(F32)
    return offset, allowed


def gather_weights(own, s, zh, zl, y):
    rows, _, c = own.shape
    outer = lax.axis_size("zh")
    halves = own.reshape(rows, 2, 2, c)
    kept = pick(halves, s, 1)
    recv = swap(pick(halves, 1 - s, 1), "s")
    out = []
    for layer in range(2):
        mine = jnp.where(s == layer, kept, recv)
        a = in_order(pick(mine, zl, 1), swap(pick(mine, 1 - zl, 1), "zl"), zl, 0)
        pieces = [a] + [swap(a, "zh", k) for k in range(1, outer)]
        pieces = jnp.stack([jnp.stack([p, swap(p, "y")]) for p in pieces])
        full = jnp.stack(
            [jnp.stack([pick(pick(pieces, zh ^ i, 0), y ^ j, 0) for j in range(2)], axis=1) for i in range(outer)]
        )
        out.append(full.reshape(outer * 4 * rows, c))
    return out


def scatter_grads(grads, s, zh, zl, y):
    outer = lax.axis_size("zh")
    c = grads[0].shape[1]
    rows = grads[0].shape[0] // (outer * 4)
    quarters = []
    for g in grads:
        v = g.reshape(outer, 2, 2, rows, c)
        v = pick(v, y, 2).astype(F32) + swap(pick(v, 1 - y, 2), "y").astype(F32)
        total = pick(v, zh, 0)
        v = v.astype(BF)
        for k in range(1, outer):
            total = total + swap(pick(v, zh ^ k, 0), "zh", k).astype(F32)
        total = total.astype(BF)
        quarters.append(in_order(pick(total, zl, 0), swap(pick(total, 1 - zl, 0), "zl"), zl, 1))
    mine = jnp.where(s == 0, quarters[0], quarters[1])
    other = jnp.where(s == 0, quarters[1], quarters[0])
    return in_order(mine, swap(other, "s"), s, 1).reshape(rows, 4, c).astype(F32)


def shards(x_in, cotangent, layout, w_qkv, b_qv, w_out, w_fc1, b_fc1, w_fc2, gains, biases):
    s, zh, zl, y, t = (lax.axis_index(a) for a in ("s", "zh", "zl", "y", "t"))
    mb, rows_mb, width = x_in.shape
    wrows = w_out.shape[1]
    block = w_out.shape[2]
    hid = w_fc1.shape[2]
    cq, hq = block // 4, hid // 4
    groups = mb * rows_mb // GROUP
    total_rows = 2 * mb * rows_mb
    share = rows_mb // 4

    att_own = jnp.concatenate(
        [w_qkv[0].reshape(wrows, 3, 4, cq).transpose(0, 2, 1, 3).reshape(wrows, 4, 3 * cq), w_out[0].reshape(wrows, 4, cq)],
        axis=2,
    )
    ff_own = jnp.concatenate([w_fc1[0].reshape(wrows, 4, hq), w_fc2[0].reshape(wrows, 4, hq)], axis=2)
    w_att = gather_weights(att_own, s, zh, zl, y)
    w_ff = gather_weights(ff_own, s, zh, zl, y)

    small_sizes = (2 * block, hid, 2 * width, 4 * width)
    small = jnp.concatenate([b_qv[0].reshape(-1), b_fc1[0], gains[0].reshape(-1), biases[0].reshape(-1)])
    small_other = swap(small, "s")
    params = []
    for layer in range(2):
        v = jnp.where(s == layer, small, small_other)
        a, b, c, d = jnp.split(v, [small_sizes[0], sum(small_sizes[:2]), sum(small_sizes[:3])])
        quarter = s * 2 + zl
        params.append(
            (
                pick(a.reshape(2, 4, cq), quarter, 1),
                pick(b.reshape(4, hq), quarter, 0),
                c.reshape(2, width),
                d.reshape(4, width),
            )
        )

    def from_pair(v):
        half = v.shape[-1] // 2
        part = lax.dynamic_slice_in_dim(v, t * half, half, v.ndim - 1)
        got = swap(part, "zl")
        other = swap(got, "t")
        other = jnp.where(t == 0, jnp.concatenate([got, other], -1), jnp.concatenate([other, got], -1))
        return in_order(v, other, zl, 0)

    x0 = from_pair(x_in)
    cot = from_pair(cotangent)
    segments = in_order(layout, swap(layout, "zl"), zl, 0).reshape(-1, GROUP)
    offset, allowed = jax.vmap(geometry)(segments)
    local_heads = cq // HEAD_DIM
    head_ids = t * (block // HEAD_DIM) + (s * 2 + zl) * local_heads + jnp.arange(local_heads, dtype=jnp.int32)
    slopes = jnp.exp2(-8.0 * (head_ids + 1).astype(F32) / HEADS)
    score_scale = float(HEAD_DIM) ** -0.5

    def own_rows(v):
        v = pick(v.reshape(2, mb, 2, 2, share, width), zl, 0)
        return pick(pick(v, s, 1), t, 1).astype(F32)

    def reduce_rows(p):
        v = p.reshape(2, mb, 2, 2, share, width)
        v = pick(v, t, 3) + swap(pick(v, 1 - t, 3).astype(BF), "t").astype(F32)
        v = pick(v, s, 2) + swap(pick(v, 1 - s, 2).astype(BF), "s").astype(F32)
        return pick(v, zl, 0) + swap(pick(v, 1 - zl, 0).astype(BF), "zl").astype(F32)

    def spread_local(v):
        v = in_order(v, swap(v, "s"), s, 1)
        return in_order(v, swap(v, "t"), t, 2)

    def spread_rows(v):
        v = in_order(v, swap(v, "zl"), zl, 0)
        v = in_order(v, swap(v, "s"), s, 2)
        return in_order(v, swap(v, "t"), t, 3).reshape(total_rows, width)

    def heads_of(v):
        return v.reshape(2 * groups, GROUP, local_heads, HEAD_DIM)

    def scores_of(q, k):
        sc = jnp.einsum("gqhd,gkhd->ghqk", heads_of(q), heads_of(k), preferred_element_type=F32) * score_scale
        sc = sc - slopes[None, :, None, None] * offset[:, None]
        return jnp.where(allowed[:, None], sc, -1000000000.0)

    def forward(x, layer):
        b_q, b_up, gain, shift = params[layer]
        wa, wf = w_att[layer], w_ff[layer]
        xf = x.reshape(total_rows, width).astype(F32)
        vh, _ = normalize(xf)
        normed = (vh * gain[0] + shift[0]).astype(BF)
        proj = dot(normed, wa[:, : 3 * cq])
        q = (proj[:, :cq] + b_q[0]).astype(BF)
        k = proj[:, cq : 2 * cq].astype(BF)
        v = (proj[:, 2 * cq :] + b_q[1]).astype(BF)
        sc = scores_of(q, k)
        top = jnp.max(sc, axis=-1, keepdims=True)
        lifted = jnp.exp(sc - top)
        total = jnp.sum(lifted, axis=-1, keepdims=True)
        probs = (lifted / total).astype(BF)
        log_total = top + jnp.log(total)
        mixed = jnp.einsum("ghqk,gkhd->gqhd", probs, heads_of(v), preferred_element_type=F32)
        mixed = mixed.reshape(total_rows, cq).astype(BF)
        branch = reduce_rows(dot_t(mixed, wa[:, 3 * cq :]))
        hidden = own_rows(x) + branch + shift[2]
        vh2, _ = normalize(hidden)
        normed_two = spread_rows((vh2 * gain[1] + shift[1]).astype(BF))
        upward = dot(normed_two, wf[:, :hq]) + b_up
        act = gelu_parts(upward)[0].astype(BF)
        down = reduce_rows(dot_t(act, wf[:, hq:]))
        result = (hidden + down + shift[3]).astype(BF)
        return result, (x, normed, q, k, v, mixed, log_total, hidden, normed_two, upward, act)

    out0, stash0 = forward(x0, 0)
    x1 = spread_rows(out0)
    out1, stash1 = forward(x1, 1)
    sec0 = pick(x1.reshape(2, mb, rows_mb, width), zl, 0)
    sec1 = spread_local(out1).reshape(mb, rows_mb, width)
    section_outputs = jnp.where(s == 0, sec0, sec1)[None]

    def ln_back(e, v, gain):
        vh, r = normalize(v)
        f = e * gain
        grad = r * (f - jnp.mean(f, -1, keepdims=True) - vh * jnp.mean(f * vh, -1, keepdims=True))
        return grad, jnp.sum(e * vh, (0, 1)), jnp.sum(e, (0, 1))

    def backward(g, stash, layer):
        b_q, b_up, gain, shift = params[layer]
        wa, wf = w_att[layer], w_ff[layer]
        x, normed, q, k, v, mixed, log_total, hidden, normed_two, upward, act = stash
        g = g.reshape(total_rows, width)
        g_own = own_rows(g)
        slope_up = gelu_parts(upward)[1]
        grad_up = (dot(g, wf[:, hq:]) * slope_up).astype(BF)
        e2 = reduce_rows(dot_t(grad_up, wf[:, :hq]))
        terms_ff = jnp.concatenate([row_dot(normed_two, grad_up), row_dot(g, act)], axis=1).astype(BF)
        grad_ln2, gain2, shift2 = ln_back(e2, hidden, gain[1])
        grad_hidden = g_own + grad_ln2
        grad_branch = spread_rows(grad_hidden.astype(BF))
        grad_mixed = dot(grad_branch, wa[:, 3 * cq :]).astype(BF)
        probs = jnp.exp(scores_of(q, k) - log_total)
        gm = heads_of(grad_mixed)
        grad_probs = jnp.einsum("gqhd,gkhd->ghqk", gm, heads_of(v), preferred_element_type=F32)
        grad_v = jnp.einsum("ghqk,gqhd->gkhd", probs.astype(BF), gm, preferred_element_type=F32)
        centre = jnp.sum(probs * grad_probs, axis=-1, keepdims=True)
        grad_sc = (probs * (grad_probs - centre)).astype(BF)
        grad_q = jnp.einsum("ghqk,gkhd->gqhd", grad_sc, heads_of(k), preferred_element_type=F32) * score_scale
        grad_k = jnp.einsum("ghqk,gqhd->gkhd", grad_sc, heads_of(q), preferred_element_type=F32) * score_scale
        grad_proj = jnp.concatenate([a.reshape(total_rows, cq).astype(BF) for a in (grad_q, grad_k, grad_v)], axis=1)
        e1 = reduce_rows(dot_t(grad_proj, wa[:, : 3 * cq]))
        terms_att = jnp.concatenate([row_dot(normed, grad_proj), row_dot(grad_branch, mixed)], axis=1).astype(BF)
        grad_ln1, gain1, shift1 = ln_back(e1, own_rows(x), gain[0])
        grad_in = (grad_hidden + grad_ln1).astype(BF)
        rows_small = jnp.stack([gain1, gain2, shift1, shift2, jnp.sum(grad_hidden, (0, 1)), jnp.sum(g_own, (0, 1))])
        sums = jnp.sum(grad_proj.astype(F32), 0)
        cols_small = (jnp.stack([sums[:cq], sums[2 * cq :]]), jnp.sum(grad_up.astype(F32), 0))
        return grad_in, terms_att, terms_ff, rows_small, cols_small

    gin1, ta1, tf1, rs1, cs1 = backward(cot, stash1, 1)
    g0 = spread_rows(gin1)
    gin0, ta0, tf0, rs0, cs0 = backward(g0, stash0, 0)
    grad_ff = scatter_grads((tf0, tf1), s, zh, zl, y)
    grad_att = scatter_grads((ta0, ta1), s, zh, zl, y)
    in1 = pick(g0.reshape(2, mb, rows_mb, width), zl, 0)
    in0 = spread_local(gin0).reshape(mb, rows_mb, width)
    input_grads = jnp.where(s == 0, in0, in1)[None]

    pieces = []
    for rs, (cqv, cup) in ((rs0, cs0), (rs1, cs1)):
        place = (t * 4 + s * 2 + zl).astype(jnp.int32)
        wide_qv = lax.dynamic_update_slice(jnp.zeros((2, 8, cq), F32), cqv[:, None], (0, place, 0))
        wide_up = lax.dynamic_update_slice(jnp.zeros((8, hq), F32), cup[None], (place, 0))
        pieces.append(jnp.concatenate([rs.reshape(-1), wide_qv.reshape(-1), wide_up.reshape(-1)]))
    total = lax.psum(jnp.stack(pieces), ("s", "zh", "zl", "y", "t"))
    total = pick(total, s, 0)
    grad_gains = total[: 2 * width].reshape(1, 2, width)
    grad_biases = total[2 * width : 6 * width].reshape(1, 4, width)
    grad_b_qv = pick(total[6 * width : 6 * width + 16 * cq].reshape(1, 2, 2, 4 * cq), t, 2)
    grad_b_fc1 = pick(total[6 * width + 16 * cq :].reshape(1, 2, 4 * hq), t, 1)

    g_qkv = grad_att[:, :, : 3 * cq].reshape(wrows, 4, 3, cq).transpose(0, 2, 1, 3).reshape(1, wrows, 3, block)
    g_out = grad_att[:, :, 3 * cq :].reshape(1, wrows, block)
    g_fc1 = grad_ff[:, :, :hq].reshape(1, wrows, hid)
    g_fc2 = grad_ff[:, :, hq:].reshape(1, wrows, hid)
    return section_outputs, input_grads, g_qkv, grad_b_qv, g_out, g_fc1, grad_b_fc1, g_fc2, grad_gains, grad_biases


def solution(mesh):
    n_s, n_dp, n_t = mesh.shape["section"], mesh.shape["dp"], mesh.shape["tensor"]
    fine = Mesh(mesh.devices.reshape(n_s, n_dp // 4, 2, 2, n_t), ("s", "zh", "zl", "y", "t"))
    return jax.shard_map(
        shards,
        mesh=fine,
        in_specs=(
            P(None, DP, None),
            P(None, DP, None),
            P(None, DP),
            P("s", DP, None, "t"),
            P("s", None, "t"),
            P("s", DP, "t"),
            P("s", DP, "t"),
            P("s", "t"),
            P("s", DP, "t"),
            P("s", None, None),
            P("s", None, None),
        ),
        out_specs=(
            P("s", None, DP, None),
            P("s", None, DP, None),
            P("s", DP, None, "t"),
            P("s", None, "t"),
            P("s", DP, "t"),
            P("s", DP, "t"),
            P("s", "t"),
            P("s", DP, "t"),
            P("s", None, None),
            P("s", None, None),
        ),
        check_vma=False,
    )
```

```python
import functools

import jax
import jax.numpy as jnp
from jax import lax
from jax.experimental import pallas as pl
from jax.experimental.pallas import tpu as pltpu
from jax.sharding import Mesh, PartitionSpec as P

HEADS = 32
HEAD_DIM = 64
GROUP = 256
EPS = 1e-05
BF = jnp.bfloat16
F32 = jnp.float32
DP = ("zh", "zl", "y")
MESH = pl.DeviceIdType.MESH
REL = ((1, 1), (0, 1), (1, 0), (0, 0))
CHUNK = 16
FAR = 1e30


def dot(a, b):
    return jnp.dot(a, b, preferred_element_type=F32)


def dot_t(a, b):
    return lax.dot_general(a, b, (((1,), (1,)), ((), ())), preferred_element_type=F32)


def row_dot(a, b):
    return lax.dot_general(a, b, (((0,), (0,)), ((), ())), preferred_element_type=F32)


def normalize(v):
    centred = v - jnp.mean(v, axis=-1, keepdims=True)
    scale = lax.rsqrt(jnp.mean(centred * centred, axis=-1, keepdims=True) + EPS)
    return centred * scale, scale


def geometry(segment):
    length = segment.shape[0]
    places = jnp.arange(length, dtype=jnp.int32)
    same_seg = segment[:, None] == segment[None, :]
    starts = jnp.min(jnp.where(same_seg, places[None, :], length), axis=1)
    prompt_len = jnp.sum((segment == 0).astype(jnp.int32))
    position = jnp.where(segment == 0, places, prompt_len + places - starts)
    allowed = (position[None, :] <= position[:, None]) & ((segment[None, :] == 0) | same_seg)
    offset = (position[:, None] - position[None, :]).astype(F32)
    return jnp.where(allowed, offset, FAR)


class Place:
    def __init__(self):
        self.s, self.zh, self.zl, self.y, self.t = (lax.axis_index(a) for a in ("s", "zh", "zl", "y", "t"))
        self.outer = lax.axis_size("zh")
        self.far = self.outer * 2

    def block(self, zh, zl, y):
        return (zh * 2 + zl) * 2 + y

    def meet(self):
        barrier = pltpu.get_barrier_semaphore()
        others = [{"t": self.t ^ 1}, {"y": self.y ^ 1}]
        others += [{"s": self.s ^ 1, "zl": self.zl ^ k} for k in range(2)]
        others += [{"zh": self.zh ^ (k // 2), "zl": self.zl ^ (k % 2)} for k in range(1, self.far)]
        for other in others:
            pl.semaphore_signal(barrier, inc=1, device_id=other, device_id_type=MESH)
        pl.semaphore_wait(barrier, len(others))


def remote(src, dst, send, recv, **where):
    return pltpu.make_async_remote_copy(
        src_ref=src, dst_ref=dst, send_sem=send, recv_sem=recv, device_id=where, device_id_type=MESH
    )


class Sums:
    def __init__(self, me, part, full, tbuf, rbuf, sems):
        self.me, self.part, self.full, self.tbuf, self.rbuf, self.sems = me, part, full, tbuf, rbuf, sems
        s, zl, t = me.s, me.zl, me.t
        self.core, self.chip = [], []
        for i, (ds, dzl) in enumerate(REL):
            self.core.append(
                remote(part.at[zl ^ dzl, :, s ^ ds, t ^ 1], tbuf.at[i], sems.at[0, i], sems.at[1, i], t=t ^ 1)
            )
        for i, (ds, dzl) in enumerate(REL[:3]):
            self.chip.append(
                remote(
                    part.at[zl ^ dzl, :, s ^ ds, t], rbuf.at[i], sems.at[2, i], sems.at[3, i], s=s ^ ds, zl=zl ^ dzl
                )
            )

    def to_core(self, *which):
        for i in which:
            self.core[i].start()

    def to_chip(self, *which):
        me, part, tbuf = self.me, self.part, self.tbuf
        for i in which:
            ds, dzl = REL[i]
            self.core[i].wait_recv()
            a, b = me.zl ^ dzl, me.s ^ ds
            mb, share = part.shape[1], part.shape[4]

            def add(j, carry, i=i, a=a, b=b, share=share):
                m, r = j // (share // CHUNK), pl.ds(pl.multiple_of((j % (share // CHUNK)) * CHUNK, CHUNK), CHUNK)
                v = part[a, m, b, me.t, r].astype(F32) + tbuf[i, m, r].astype(F32)
                part[a, m, b, me.t, r] = v.astype(BF)
                return carry

            lax.fori_loop(0, mb * share // CHUNK, add, 0)
            self.chip[i].start()

    def finish(self, row_fn):
        me, part, tbuf, rbuf, full = self.me, self.part, self.tbuf, self.rbuf, self.full
        self.core[3].wait_recv()
        for c in self.chip:
            c.wait_recv()
        mb, share = part.shape[1], part.shape[4]

        def add(j, carry):
            m, r = j // (share // CHUNK), pl.ds(pl.multiple_of((j % (share // CHUNK)) * CHUNK, CHUNK), CHUNK)
            v = part[me.zl, m, me.s, me.t, r].astype(F32) + tbuf[3, m, r].astype(F32)
            v = v + rbuf[0, m, r].astype(F32) + rbuf[1, m, r].astype(F32) + rbuf[2, m, r].astype(F32)
            full[me.zl, m, me.s, me.t, r] = row_fn(m, r, v)
            return carry

        lax.fori_loop(0, mb * share // CHUNK, add, 0)
        for c in self.core + self.chip:
            c.wait_send()

    def spread(self):
        me, full, sems = self.me, self.full, self.sems
        own = full.at[me.zl, :, me.s, me.t]
        self.out = [
            remote(own, own, sems.at[4, i], sems.at[5, i], s=me.s ^ ds, zl=me.zl ^ dzl)
            for i, (ds, dzl) in enumerate(REL[:3])
        ]
        for c in self.out:
            c.start()
        self.cross = [None] * 4
        self.forward(3, own)

    def forward(self, i, piece):
        me, sems = self.me, self.sems
        self.cross[i] = remote(piece, piece, sems.at[6, i], sems.at[7, i], t=me.t ^ 1)
        self.cross[i].start()

    def collect(self):
        me, full = self.me, self.full
        for i in (2, 1, 0):
            ds, dzl = REL[i]
            self.out[i].wait_recv()
            self.forward(i, full.at[me.zl ^ dzl, :, me.s ^ ds, me.t])
        for c in self.cross:
            c.wait_recv()
        for c in self.cross + self.out:
            c.wait_send()


def sums_scratch(mb, share, width):
    return [
        pltpu.VMEM((2, mb, 2, 2, share, width), BF),
        pltpu.VMEM((4, mb, share, width), BF),
        pltpu.VMEM((3, mb, share, width), BF),
        pltpu.SemaphoreType.DMA((8, 4)),
    ]


class Fetch:
    def __init__(self, me, layer, pairs, sems):
        self.me, self.pairs = me, pairs
        self.first, self.far, self.near = [], [], []
        home = me.block(me.zh, me.zl, me.y)
        for p, (half, whole) in enumerate(pairs):
            c = whole.shape[-1]
            src = lambda q, half=half, c=c: half.at[layer, :, :, pl.ds(pl.multiple_of(q * c, c), c)]
            dst = whole.at[:, home]
            sem = lambda a, k, p=p: sems.at[p, a, k]
            self.first.append(pltpu.make_async_copy(src(me.zl), dst, sem(4, 0)))
            for k in reversed(range(1, me.far)):
                zh, zl = me.zh ^ (k // 2), me.zl ^ (k % 2)
                self.far.append((p, k, remote(src(zl), dst, sem(0, k), sem(1, k), zh=zh, zl=zl)))
            self.near.append(remote(src(me.zl), dst, sem(2, 0), sem(3, 0), y=me.y ^ 1))
        self.sem = sems

    def start(self):
        for c in self.first:
            c.start()
        for _, _, c in self.far:
            c.start()
        for c in self.near:
            c.start()

    def pass_on(self, lo=0, hi=None):
        me = self.me
        for p, k, c in self.far[lo:hi]:
            c.wait_recv()
            whole = self.pairs[p][1]
            piece = whole.at[:, me.block(me.zh ^ (k // 2), me.zl ^ (k % 2), me.y)]
            on = remote(piece, piece, self.sem.at[p, 2, k], self.sem.at[p, 3, k], y=me.y ^ 1)
            on.start()
            self.near.append(on)

    def finish(self):
        for c in self.first:
            c.wait()
        for _, _, c in self.far:
            c.wait_send()
        for c in self.near:
            c.wait()


def fetch_sems(pairs, far):
    return pltpu.SemaphoreType.DMA((pairs, 5, far))


class Deliver:
    def __init__(self, me, quads, sems):
        self.me, self.quads, self.sems = me, quads, sems
        self.near, self.far = [], []
        for p, (terms, ybuf, zbuf, out) in enumerate(quads):
            for k in reversed(range(me.far)):
                zh, zl = me.zh ^ (k // 2), me.zl ^ (k % 2)
                src = terms.at[:, me.block(zh, zl, me.y ^ 1)]
                self.near.append((p, k, remote(src, ybuf.at[:, k], sems.at[p, 0, k], sems.at[p, 1, k], y=me.y ^ 1)))
                if k:
                    self.far.append(
                        remote(ybuf.at[:, k], zbuf.at[:, k - 1], sems.at[p, 2, k], sems.at[p, 3, k], zh=zh, zl=zl)
                    )

    def start(self):
        for _, _, c in self.near:
            c.start()

    def add(self, lo=0, hi=None):
        me = self.me
        for p, k, c in self.near[lo:hi]:
            terms, ybuf, zbuf, out = self.quads[p]
            c.wait_recv()
            kinds, rows = ybuf.shape[0], ybuf.shape[2]
            b = me.block(me.zh ^ (k // 2), me.zl ^ (k % 2), me.y)

            def step(j, carry, k=k, b=b, rows=rows, terms=terms, ybuf=ybuf):
                m, r = j // (rows // CHUNK), pl.ds(pl.multiple_of((j % (rows // CHUNK)) * CHUNK, CHUNK), CHUNK)
                ybuf[m, k, r] = (ybuf[m, k, r].astype(F32) + terms[m, b, r].astype(F32)).astype(BF)
                return carry

            lax.fori_loop(0, kinds * rows // CHUNK, step, 0)
            if k:
                self.far[p * (me.far - 1) + (me.far - 1 - k)].start()

    def finish(self):
        me = self.me
        for c in self.far:
            c.wait_recv()
        for p, (terms, ybuf, zbuf, out) in enumerate(self.quads):
            kinds, rows, c = ybuf.shape[0], ybuf.shape[2], ybuf.shape[3]

            def step(j, carry, rows=rows, c=c, ybuf=ybuf, zbuf=zbuf, out=out):
                m, r = j // (rows // CHUNK), pl.ds(pl.multiple_of((j % (rows // CHUNK)) * CHUNK, CHUNK), CHUNK)
                same, other = ybuf[m, 0, r].astype(F32), zbuf[m, 0, r].astype(F32)
                for k in range(2, me.far):
                    if k % 2:
                        other = other + zbuf[m, k - 1, r].astype(F32)
                    else:
                        same = same + zbuf[m, k - 1, r].astype(F32)
                out[me.zl, m, r] = same.astype(BF)
                out[me.zl ^ 1, m, r] = other.astype(BF)
                return carry

            lax.fori_loop(0, kinds * rows // CHUNK, step, 0)
        for _, _, c in self.near:
            c.wait_send()
        for c in self.far:
            c.wait_send()


def deliver_sems(pairs, far):
    return pltpu.SemaphoreType.DMA((pairs, 4, far))


VM = pl.BlockSpec(memory_space=pltpu.VMEM)
SM = pl.BlockSpec(memory_space=pltpu.SMEM)
AN = pl.BlockSpec(memory_space=pl.ANY)


def call(body, cid, ins, in_specs, outs, out_specs, scratch, flops=0):
    return pl.pallas_call(
        body,
        out_shape=[jax.ShapeDtypeStruct(sh, dt) for sh, dt in outs],
        in_specs=in_specs,
        out_specs=out_specs,
        scratch_shapes=scratch,
        compiler_params=pltpu.CompilerParams(
            collective_id=cid, has_side_effects=True, vmem_limit_bytes=60 * 1024 * 1024
        ),
    )(*ins)


def fetch_first(qkv, o, up, dn, x_in, cot, qkv_h, o_h, up_h, dn_h, w_qkv, w_o, x_all, c_all, sems, xsems, fsems):
    me = Place()
    me.meet()
    other, jobs = me.s ^ 1, []
    for p, (own, half) in enumerate(((qkv, qkv_h), (o, o_h), (up, up_h), (dn, dn_h))):
        w = own.shape[-1] // 2
        cols = lambda q, w=w: pl.ds(pl.multiple_of(q * w, w), w)
        there = remote(own.at[:, :, cols(other)], half.at[me.s], sems.at[0, p], sems.at[1, p], s=other)
        here = pltpu.make_async_copy(own.at[:, :, cols(me.s)], half.at[me.s], sems.at[2, p])
        there.start()
        here.start()
        jobs.append((there, here))
    moved = []
    for a, (own, full) in enumerate(((x_in, x_all), (cot, c_all))):
        local = pltpu.make_async_copy(own, full.at[me.zl], xsems.at[a, 4])
        across = remote(own.at[:, :, me.t], full.at[me.zl, :, :, me.t], xsems.at[a, 0], xsems.at[a, 1], zl=me.zl ^ 1)
        local.start()
        across.start()
        moved.append([local, across, full])
    for there, here in jobs[:2]:
        here.wait()
        there.wait_recv()
    pack = Fetch(me, 0, ((qkv_h, w_qkv), (o_h, w_o)), fsems)
    pack.start()
    crossed = []
    for a, (local, across, full) in enumerate(moved):
        across.wait_recv()
        piece = full.at[me.zl ^ 1, :, :, me.t]
        c = remote(piece, piece, xsems.at[a, 2], xsems.at[a, 3], t=me.t ^ 1)
        c.start()
        crossed.append(c)
    pack.pass_on()
    pack.finish()
    for there, here in jobs[2:]:
        here.wait()
        there.wait_recv()
    for there, _ in jobs:
        there.wait_send()
    for (local, across, _), c in zip(moved, crossed):
        local.wait()
        across.wait_send()
        c.wait()


def rows_of(ref, a, m):
    v = ref[a, m]
    return v.reshape(-1, v.shape[-1])


def put_rows(ref, a, m, v):
    ref[a, m] = v.reshape(ref.shape[2:])


def group_place(me, i, mb):
    return (me.zl ^ 1) if i < mb else me.zl, i % mb


def norm_rows(src, dst, a, m, gain, shift):
    share = src.shape[4]

    def step(j, carry):
        q, r = j // (share // CHUNK), pl.ds(pl.multiple_of((j % (share // CHUNK)) * CHUNK, CHUNK), CHUNK)
        vh, _ = normalize(src[a, m, q // 2, q % 2, r].astype(F32))
        dst[a, m, q // 2, q % 2, r] = (vh * gain + shift).astype(BF)
        return carry

    lax.fori_loop(0, 4 * share // CHUNK, step, 0)


def lanes(width):
    return lax.broadcasted_iota(jnp.int32, (1, width), 1)


def head_mask(h):
    return (lanes(2 * HEAD_DIM) // HEAD_DIM) == h


def softmax_parts(q, k, pen, slope):
    sc = dot_t(q, k) * (float(HEAD_DIM) ** -0.5) - slope * pen
    lifted = jnp.exp(sc - jnp.max(sc, axis=-1, keepdims=True))
    return lifted / jnp.sum(lifted, axis=-1, keepdims=True)


def att_forward(
    layer, has_fetch, x, wqkv, wo, bias, vecs, slopes, pen, *rest
):
    rest = list(rest)
    n_in = 2 if has_fetch else 0
    halves, rest = rest[:n_in], rest[n_in:]
    normed, proj, mixed, hidden, full = rest[:5]
    wholes, rest = rest[5 : 5 + n_in], rest[5 + n_in :]
    part, tbuf, rbuf, sems = rest[:4]
    me = Place()
    me.meet()
    fetch = None
    if has_fetch:
        fetch = Fetch(me, has_fetch[0], tuple(zip(halves, wholes)), rest[4])
        fetch.start()
    sums = Sums(me, part, full, tbuf, rbuf, sems)
    mb = x.shape[1]
    cq = wo.shape[-1]

    def group(a, m):
        norm_rows(x, normed, a, m, vecs[0:1], vecs[1:2])
        nv = rows_of(normed, a, m)
        for k in range(3):
            v = dot(nv, wqkv[k])
            if k == 0:
                v = v + bias[0:1]
            if k == 2:
                v = v + bias[1:2]
            proj[k, a, m] = v.astype(BF)
        pv = pen[a, m]
        for pair in range(cq // (2 * HEAD_DIM)):
            cols = slice(pair * 2 * HEAD_DIM, (pair + 1) * 2 * HEAD_DIM)
            q, k, v = proj[0, a, m, :, cols], proj[1, a, m, :, cols], proj[2, a, m, :, cols]
            got = []
            for h in range(2):
                probs = softmax_parts(jnp.where(head_mask(h), q, jnp.zeros_like(q)), k, pv, slopes[pair * 2 + h])
                got.append(dot(probs.astype(BF), v))
            mixed[a, m, :, cols] = jnp.where(head_mask(0), got[0], got[1]).astype(BF)
        put_rows(part, a, m, dot_t(mixed[a, m], wo[...]).astype(BF))

    lax.fori_loop(0, mb, lambda m, c: (group(me.zl ^ 1, m), c)[1], 0)
    sums.to_core(0, 1)
    lax.fori_loop(0, mb, lambda m, c: (group(me.zl, m), c)[1], 0)
    sums.to_core(2, 3)
    sums.to_chip(0, 1, 2)
    if fetch:
        fetch.pass_on(0, 3)

    def rows(m, r, v):
        hid = x[me.zl, m, me.s, me.t, r].astype(F32) + v + vecs[4:5]
        hidden[m, r] = hid
        vh, _ = normalize(hid)
        return (vh * vecs[2:3] + vecs[3:4]).astype(BF)

    sums.finish(rows)
    sums.spread()
    sums.collect()
    if fetch:
        fetch.pass_on(3)
        fetch.finish()


def ff_forward(layer, has_fetch, x, wup, wdn, bias, vecs, hidden, *rest):
    rest = list(rest)
    n_in = 2 if has_fetch else 0
    halves, rest = rest[:n_in], rest[n_in:]
    upward, act, full = rest[:3]
    wholes, rest = rest[3 : 3 + n_in], rest[3 + n_in :]
    part, tbuf, rbuf, sems = rest[:4]
    me = Place()
    me.meet()
    fetch = None
    if has_fetch:
        fetch = Fetch(me, has_fetch[0], tuple(zip(halves, wholes)), rest[4])
        fetch.start()
    sums = Sums(me, part, full, tbuf, rbuf, sems)
    mb = x.shape[1]
    hq = wup.shape[-1]
    tile = 512

    def group(a, m):
        nv = rows_of(x, a, m)
        for j in range(hq // tile):
            cols = slice(j * tile, (j + 1) * tile)
            u = dot(nv, wup[:, cols]) + bias[:, cols]
            upward[a, m, :, cols] = u
            act[a, m, :, cols] = (u * (0.5 + 0.5 * lax.erf(u * (0.5**0.5)))).astype(BF)
        put_rows(part, a, m, dot_t(act[a, m], wdn[...]).astype(BF))

    lax.fori_loop(0, mb, lambda m, c: (group(me.zl ^ 1, m), c)[1], 0)
    sums.to_core(0, 1)
    lax.fori_loop(0, mb, lambda m, c: (group(me.zl, m), c)[1], 0)
    sums.to_core(2, 3)
    sums.to_chip(0, 1, 2)
    if fetch:
        fetch.pass_on(0, 3)
    sums.finish(lambda m, r, v: (hidden[m, r] + v + vecs[5:6]).astype(BF))
    sums.spread()
    sums.collect()
    if fetch:
        fetch.pass_on(3)
        fetch.finish()


def ln_back(e, v, gain):
    vh, r = normalize(v)
    f = e * gain
    grad = r * (f - jnp.mean(f, -1, keepdims=True) - vh * jnp.mean(f * vh, -1, keepdims=True))
    return grad, e * vh


def fold(v):
    return v[:8] + v[8:]


def ff_backward(layer, has_deliver, g, normed_two, act, upward, wup, wdn, vecs, hidden, *rest):
    rest = list(rest)
    n_in = has_deliver
    terms, rest = rest[:n_in], rest[n_in:]
    g_up, g_dn, grad_hidden, small, small_up, full = rest[:6]
    outs, rest = rest[6 : 6 + n_in], rest[6 + n_in :]
    part, tbuf, rbuf, sems, gu = rest[:5]
    me = Place()
    me.meet()
    deliver = None
    if n_in:
        bufs = rest[5:]
        deliver = Deliver(me, [(terms[i], bufs[2 * i], bufs[2 * i + 1], outs[i]) for i in range(n_in)], bufs[-1])
        deliver.start()
    sums = Sums(me, part, full, tbuf, rbuf, sems)
    mb = g.shape[1]
    hq = wup.shape[-1]
    tile = 512
    small[...] = jnp.zeros_like(small)
    small_up[...] = jnp.zeros_like(small_up)

    def group(a, m):
        gv = rows_of(g, a, m)
        for j in range(hq // tile):
            cols = slice(j * tile, (j + 1) * tile)
            u = upward[a, m, :, cols]
            slope = 0.5 + 0.5 * lax.erf(u * (0.5**0.5)) + u * (jnp.exp(-0.5 * u * u) * 0.3989422804014327)
            v = (dot(gv, wdn[:, cols]) * slope).astype(BF)
            gu[a, m, :, cols] = v
            small_up[:, cols] += jnp.sum(v.astype(F32).reshape(-1, 8, tile), axis=0)
        put_rows(part, a, m, dot_t(gu[a, m], wup[...]).astype(BF))

    lax.fori_loop(0, mb, lambda m, c: (group(me.zl ^ 1, m), c)[1], 0)
    sums.to_core(0, 1)
    lax.fori_loop(0, mb, lambda m, c: (group(me.zl, m), c)[1], 0)
    sums.to_core(2, 3)
    sums.to_chip(0, 1, 2)

    def flat(ref):
        v = ref[...]
        return v.reshape(-1, v.shape[-1])

    nt = 256
    width = g.shape[-1]

    def product(dst, left, right):
        def step(j, carry):
            cols = pl.ds(pl.multiple_of(j * nt, nt), nt)
            lv = left[:, :, :, :, :, cols].reshape(-1, nt)
            dst[cols] = row_dot(lv, flat(right)).astype(BF)
            return carry

        lax.fori_loop(0, width // nt, step, 0)

    product(g_dn, g, act)

    def rows(m, r, e):
        grad, ev = ln_back(e, hidden[m, r], vecs[2:3])
        go = g[me.zl, m, me.s, me.t, r].astype(F32)
        grad = go + grad
        grad_hidden[m, r] = grad
        small[0] += fold(ev)
        small[1] += fold(e)
        small[2] += fold(grad)
        small[3] += fold(go)
        return grad.astype(BF)

    sums.finish(rows)
    sums.spread()
    if deliver:
        deliver.add()
    product(g_up, normed_two, gu)
    sums.collect()
    if deliver:
        deliver.finish()


def att_backward(
    layer, has_deliver, gb, x, normed, proj, mixed, wqkv, wo, vecs, slopes, pen, grad_hidden, *rest
):
    rest = list(rest)
    n_in = has_deliver
    terms, rest = rest[:n_in], rest[n_in:]
    g_qkv, g_o, small, small_p, full = rest[:5]
    outs, rest = rest[5 : 5 + n_in], rest[5 + n_in :]
    part, tbuf, rbuf, sems, gp = rest[:5]
    me = Place()
    me.meet()
    deliver = None
    if n_in:
        bufs = rest[5:]
        deliver = Deliver(me, [(terms[i], bufs[2 * i], bufs[2 * i + 1], outs[i]) for i in range(n_in)], bufs[-1])
        deliver.start()
    sums = Sums(me, part, full, tbuf, rbuf, sems)
    mb = x.shape[1]
    cq = wo.shape[-1]
    small[...] = jnp.zeros_like(small)
    small_p[...] = jnp.zeros_like(small_p)
    scale = float(HEAD_DIM) ** -0.5

    def group(a, m):
        gm_all = dot(rows_of(gb, a, m), wo[...]).astype(BF)
        pv = pen[a, m]
        for pair in range(cq // (2 * HEAD_DIM)):
            cols = slice(pair * 2 * HEAD_DIM, (pair + 1) * 2 * HEAD_DIM)
            q, k, v = proj[0, a, m, :, cols], proj[1, a, m, :, cols], proj[2, a, m, :, cols]
            gm = gm_all[:, cols]
            gq, gk, gv = [], [], []
            for h in range(2):
                zero = jnp.zeros_like(q)
                probs = softmax_parts(jnp.where(head_mask(h), q, zero), k, pv, slopes[pair * 2 + h])
                gpr = dot_t(jnp.where(head_mask(h), gm, zero), v)
                gv.append(row_dot(probs.astype(BF), gm))
                pg = probs * gpr
                gs = (pg - probs * jnp.sum(pg, axis=-1, keepdims=True)).astype(BF)
                gq.append(dot(gs, k))
                gk.append(row_dot(gs, q))
            for i, (both, f) in enumerate(((gq, scale), (gk, scale), (gv, 1.0))):
                out = (jnp.where(head_mask(0), both[0], both[1]) * f).astype(BF)
                gp[i, a, m, :, cols] = out
                small_p[i, :, cols] += jnp.sum(out.astype(F32).reshape(-1, 8, 2 * HEAD_DIM), axis=0)
        total = dot_t(gp[0, a, m], wqkv[0]) + dot_t(gp[1, a, m], wqkv[1]) + dot_t(gp[2, a, m], wqkv[2])
        put_rows(part, a, m, total.astype(BF))

    lax.fori_loop(0, mb, lambda m, c: (group(me.zl ^ 1, m), c)[1], 0)
    sums.to_core(0, 1)
    lax.fori_loop(0, mb, lambda m, c: (group(me.zl, m), c)[1], 0)
    sums.to_core(2, 3)
    sums.to_chip(0, 1, 2)

    nt = 256
    width = gb.shape[-1]

    def product(dst, left, right):
        def step(j, carry):
            cols = pl.ds(pl.multiple_of(j * nt, nt), nt)
            lv = left[:, :, :, :, :, cols].reshape(-1, nt)
            dst[cols] = row_dot(lv, right()).astype(BF)
            return carry

        lax.fori_loop(0, width // nt, step, 0)

    product(g_o, gb, lambda: mixed[...].reshape(-1, cq))

    def rows(m, r, e):
        grad, ev = ln_back(e, x[me.zl, m, me.s, me.t, r].astype(F32), vecs[0:1])
        small[0] += fold(ev)
        small[1] += fold(e)
        return (grad_hidden[m, r] + grad).astype(BF)

    sums.finish(rows)
    sums.spread()
    if deliver:
        deliver.add()
    for k in range(3):
        product(g_qkv.at[k], normed, lambda k=k: gp[k].reshape(-1, cq))
    sums.collect()
    if deliver:
        deliver.finish()


def deliver_last(n_in, *refs):
    refs = list(refs)
    terms, refs = refs[:n_in], refs[n_in:]
    outs, bufs = refs[:n_in], refs[n_in:]
    me = Place()
    me.meet()
    deliver = Deliver(me, [(terms[i], bufs[2 * i], bufs[2 * i + 1], outs[i]) for i in range(n_in)], bufs[-1])
    deliver.start()
    deliver.add()
    deliver.finish()


def swap(v, axis, offset=1):
    n = lax.axis_size(axis)
    return lax.ppermute(v, axis, [(i, i ^ offset) for i in range(n)])


def pick(v, index, dim):
    return lax.dynamic_index_in_dim(v, index, dim, keepdims=False)


def in_order(mine, other, index, dim):
    first = jnp.where(index == 0, mine, other)
    second = jnp.where(index == 0, other, mine)
    return jnp.stack([first, second], axis=dim)


def shards(x_in, cotangent, layout, w_qkv, b_qv, w_out, w_fc1, b_fc1, w_fc2, gains, biases):
    s, zh, zl, y, t = (lax.axis_index(a) for a in ("s", "zh", "zl", "y", "t"))
    outer = lax.axis_size("zh")
    far, nb = outer * 2, outer * 4
    mb, rows_mb, width = x_in.shape
    wrows = w_out.shape[1]
    block = w_out.shape[2]
    hid = w_fc1.shape[2]
    cq, hq = block // 4, hid // 4
    share = rows_mb // 4
    tokens = (2, mb, 2, 2, share, width)

    small_sizes = (2 * block, hid, 2 * width, 4 * width)
    small = jnp.concatenate([b_qv[0].reshape(-1), b_fc1[0], gains[0].reshape(-1), biases[0].reshape(-1)])
    small_other = swap(small, "s")
    quarter = s * 2 + zl
    params = []
    for layer in range(2):
        v = jnp.where(s == layer, small, small_other)
        a, b, c, d = jnp.split(v, [small_sizes[0], sum(small_sizes[:2]), sum(small_sizes[:3])])
        c, d = c.reshape(2, width), d.reshape(4, width)
        params.append(
            (
                pick(a.reshape(2, 4, cq), quarter, 1),
                pick(b.reshape(4, hq), quarter, 0)[None],
                jnp.stack([c[0], d[0], c[1], d[1], d[2], d[3]]),
            )
        )
    segments = in_order(layout, swap(layout, "zl"), zl, 0).reshape(2 * mb, rows_mb)
    pen = jax.vmap(geometry)(segments).reshape(2, mb, GROUP, GROUP)
    local_heads = cq // HEAD_DIM
    head_ids = t * (block // HEAD_DIM) + quarter * local_heads + jnp.arange(local_heads, dtype=jnp.int32)
    slopes = jnp.exp2(-8.0 * (head_ids + 1).astype(F32) / HEADS)

    qkv_own = w_qkv[0].transpose(1, 0, 2)
    res = call(
        fetch_first,
        0,
        (
            qkv_own,
            w_out,
            w_fc1,
            w_fc2,
            x_in.reshape(mb, 2, 2, share, width),
            cotangent.reshape(mb, 2, 2, share, width),
        ),
        [AN] * 6,
        [
            ((2, 3, wrows, 2 * cq), BF),
            ((2, 1, wrows, 2 * cq), BF),
            ((2, 1, wrows, 2 * hq), BF),
            ((2, 1, wrows, 2 * hq), BF),
            ((3, nb, wrows, cq), BF),
            ((1, nb, wrows, cq), BF),
            (tokens, BF),
            (tokens, BF),
        ],
        [AN] * 8,
        [pltpu.SemaphoreType.DMA((3, 4)), pltpu.SemaphoreType.DMA((2, 5)), fetch_sems(2, far)],
    )
    qkv_h, o_h, up_h, dn_h, wqkv0, wo0, x0, cot = res
    act_scratch = sums_scratch(mb, share, width)
    att_w = [((3, nb, wrows, cq), BF), ((1, nb, wrows, cq), BF)]
    ff_w = [((1, nb, wrows, hq), BF)] * 2

    def att_fwd(layer, cid, x, wqkv, wo):
        bias, _, vecs = params[layer]
        res = call(
            functools.partial(att_forward, layer, (layer,)),
            cid,
            (x, wqkv.reshape(3, width, cq), wo.reshape(width, cq), bias, vecs, slopes, pen, up_h, dn_h),
            [VM] * 5 + [SM, VM] + [AN] * 2,
            [
                (tokens, BF),
                ((3, 2, mb, rows_mb, cq), BF),
                ((2, mb, rows_mb, cq), BF),
                ((mb, share, width), F32),
                (tokens, BF),
            ]
            + ff_w,
            [VM] * 5 + [AN] * 2,
            act_scratch + [fetch_sems(2, far)],
        )
        return res

    def ff_fwd(layer, cid, nt, wup, wdn, hidden, nxt):
        _, bias, vecs = params[layer]
        ins = [nt, wup.reshape(width, hq), wdn.reshape(width, hq), bias, vecs, hidden]
        outs = [((2, mb, rows_mb, hq), F32), ((2, mb, rows_mb, hq), BF), (tokens, BF)]
        sp, so = [VM] * 6, [VM] * 3
        scratch = list(act_scratch)
        if nxt is not None:
            ins += [qkv_h, o_h]
            sp += [AN] * 2
            outs += att_w
            so += [AN] * 2
            scratch.append(fetch_sems(2, far))
        return call(
            functools.partial(ff_forward, layer, None if nxt is None else (nxt,)), cid, ins, sp, outs, so, scratch
        )

    normed0, proj0, mixed0, hidden0, nt0, wup0, wdn0 = att_fwd(0, 1, x0, wqkv0, wo0)
    upward0, act0, x1, wqkv1, wo1 = ff_fwd(0, 2, nt0, wup0, wdn0, hidden0, 1)
    normed1, proj1, mixed1, hidden1, nt1, wup1, wdn1 = att_fwd(1, 3, x1, wqkv1, wo1)
    upward1, act1, x2 = ff_fwd(1, 4, nt1, wup1, wdn1, hidden1, None)

    def deliver_parts(shapes):
        scratch = []
        for k, c in shapes:
            scratch += [pltpu.VMEM((k, far, wrows, c), BF), pltpu.VMEM((k, far - 1, wrows, c), BF)]
        return [((2, k, wrows, c), BF) for k, c in shapes], scratch + [deliver_sems(len(shapes), far)]

    att_shapes, ff_shapes = ((3, cq), (1, cq)), ((1, hq), (1, hq))

    def ff_bwd(layer, cid, g, nt, act, upward, wup, wdn, hidden, terms):
        vecs = params[layer][2]
        outs = [
            ((width, hq), BF),
            ((width, hq), BF),
            ((mb, share, width), F32),
            ((4, 8, width), F32),
            ((8, hq), F32),
            (tokens, BF),
        ]
        scratch = act_scratch + [pltpu.VMEM((2, mb, rows_mb, hq), BF)]
        d_outs, d_scratch = deliver_parts(att_shapes) if terms else ([], [])
        ins = [g, nt, act, upward, wup.reshape(width, hq), wdn.reshape(width, hq), vecs, hidden] + list(terms)
        return call(
            functools.partial(ff_backward, layer, len(terms)),
            cid,
            ins,
            [VM] * len(ins),
            outs + d_outs,
            [VM] * (len(outs) + len(d_outs)),
            scratch + d_scratch,
        )

    def att_bwd(layer, cid, gb, x, normed, proj, mixed, wqkv, wo, grad_hidden, terms):
        vecs = params[layer][2]
        outs = [((3, width, cq), BF), ((width, cq), BF), ((2, 8, width), F32), ((3, 8, cq), F32), (tokens, BF)]
        scratch = act_scratch + [pltpu.VMEM((3, 2, mb, rows_mb, cq), BF)]
        d_outs, d_scratch = deliver_parts(ff_shapes)
        ins = [
            gb, x, normed, proj, mixed, wqkv.reshape(3, width, cq), wo.reshape(width, cq), vecs, slopes, pen, grad_hidden
        ] + list(terms)
        return call(
            functools.partial(att_backward, layer, len(terms)),
            cid,
            ins,
            [VM] * 8 + [SM] + [VM] * (len(ins) - 9),
            outs + d_outs,
            [VM] * (len(outs) + len(d_outs)),
            scratch + d_scratch,
        )

    def as_ff(*terms):
        return [v.reshape(1, nb, wrows, hq) for v in terms]

    def as_att(a, b):
        return [a.reshape(3, nb, wrows, cq), b.reshape(1, nb, wrows, cq)]

    g_up1, g_dn1, gh1, sf1, su1, gb1 = ff_bwd(1, 5, cot, nt1, act1, upward1, wup1, wdn1, hidden1, ())
    g_qkv1, g_o1, sa1, sp1, g0, d_up1, d_dn1 = att_bwd(
        1, 6, gb1, x1, normed1, proj1, mixed1, wqkv1, wo1, gh1, as_ff(g_up1, g_dn1)
    )
    g_up0, g_dn0, gh0, sf0, su0, gb0, d_qkv1, d_o1 = ff_bwd(
        0, 7, g0, nt0, act0, upward0, wup0, wdn0, hidden0, as_att(g_qkv1, g_o1)
    )
    g_qkv0, g_o0, sa0, sp0, gin, d_up0, d_dn0 = att_bwd(
        0, 8, gb0, x0, normed0, proj0, mixed0, wqkv0, wo0, gh0, as_ff(g_up0, g_dn0)
    )
    d_outs, d_scratch = deliver_parts(att_shapes)
    d_qkv0, d_o0 = call(
        functools.partial(deliver_last, 2), 9, as_att(g_qkv0, g_o0), [VM] * 2, d_outs, [VM] * 2, d_scratch
    )

    def home(d0, d1):
        k, c = d0.shape[1], d0.shape[3]
        mine = jnp.where(s == 0, d0, d1)
        got = swap(jnp.where(s == 0, d1, d0), "s")
        both = in_order(mine, got, s, 0)
        return both.transpose(3, 2, 0, 1, 4).reshape(wrows, k, 4 * c).astype(F32)

    g_qkv = home(d_qkv0, d_qkv1)[None]
    g_out = home(d_o0, d_o1).reshape(1, wrows, block)
    g_fc1 = home(d_up0, d_up1).reshape(1, wrows, hid)
    g_fc2 = home(d_dn0, d_dn1).reshape(1, wrows, hid)

    sec0 = pick(x1.reshape(2, mb, rows_mb, width), zl, 0)
    sec1 = pick(x2.reshape(2, mb, rows_mb, width), zl, 0)
    section_outputs = jnp.where(s == 0, sec0, sec1)[None]
    in0 = pick(gin.reshape(2, mb, rows_mb, width), zl, 0)
    in1 = pick(g0.reshape(2, mb, rows_mb, width), zl, 0)
    input_grads = jnp.where(s == 0, in0, in1)[None]

    pieces = []
    for sf, su, sa, sp in ((sf0, su0, sa0, sp0), (sf1, su1, sa1, sp1)):
        sf, su, sa, sp = (jnp.sum(v, axis=-2) for v in (sf, su, sa, sp))
        place = (t * 4 + quarter).astype(jnp.int32)
        wide_qv = lax.dynamic_update_slice(jnp.zeros((2, 8, cq), F32), jnp.stack([sp[0], sp[2]])[:, None], (0, place, 0))
        wide_up = lax.dynamic_update_slice(jnp.zeros((8, hq), F32), su[None], (place, 0))
        rows_small = jnp.stack([sa[0], sf[0], sa[1], sf[1], sf[2], sf[3]])
        pieces.append(jnp.concatenate([rows_small.reshape(-1), wide_qv.reshape(-1), wide_up.reshape(-1)]))
    total = lax.psum(jnp.stack(pieces), ("s", "zh", "zl", "y", "t"))
    total = pick(total, s, 0)
    grad_gains = total[: 2 * width].reshape(1, 2, width)
    grad_biases = total[2 * width : 6 * width].reshape(1, 4, width)
    grad_b_qv = pick(total[6 * width : 6 * width + 16 * cq].reshape(1, 2, 2, 4 * cq), t, 2)
    grad_b_fc1 = pick(total[6 * width + 16 * cq :].reshape(1, 2, 4 * hq), t, 1)
    return section_outputs, input_grads, g_qkv, grad_b_qv, g_out, g_fc1, grad_b_fc1, g_fc2, grad_gains, grad_biases


def solution(mesh):
    n_s, n_dp, n_t = mesh.shape["section"], mesh.shape["dp"], mesh.shape["tensor"]
    fine = Mesh(mesh.devices.reshape(n_s, n_dp // 4, 2, 2, n_t), ("s", "zh", "zl", "y", "t"))
    return jax.shard_map(
        shards,
        mesh=fine,
        in_specs=(
            P(None, DP, None),
            P(None, DP, None),
            P(None, DP),
            P("s", DP, None, "t"),
            P("s", None, "t"),
            P("s", DP, "t"),
            P("s", DP, "t"),
            P("s", "t"),
            P("s", DP, "t"),
            P("s", None, None),
            P("s", None, None),
        ),
        out_specs=(
            P("s", None, DP, None),
            P("s", None, DP, None),
            P("s", DP, None, "t"),
            P("s", None, "t"),
            P("s", DP, "t"),
            P("s", DP, "t"),
            P("s", "t"),
            P("s", DP, "t"),
            P("s", None, None),
            P("s", None, None),
        ),
        check_vma=False,
    )
```

```python
import functools

import jax
import jax.numpy as jnp
from jax import lax
from jax.experimental import pallas as pl
from jax.experimental.pallas import tpu as pltpu
from jax.sharding import Mesh, PartitionSpec as P

HEADS = 32
HEAD_DIM = 64
GROUP = 256
EPS = 1e-05
BF = jnp.bfloat16
F32 = jnp.float32
DP = ("zh", "zl", "y")
MESH = pl.DeviceIdType.MESH
REL = ((1, 1), (0, 1), (1, 0), (0, 0))
CHUNK = 16
PARTS = 4
FAR = 1e30


def dot(a, b):
    return jnp.dot(a, b, preferred_element_type=F32)


def dot_t(a, b):
    return lax.dot_general(a, b, (((1,), (1,)), ((), ())), preferred_element_type=F32)


def row_dot(a, b):
    return lax.dot_general(a, b, (((0,), (0,)), ((), ())), preferred_element_type=F32)


def normalize(v):
    centred = v - jnp.mean(v, axis=-1, keepdims=True)
    scale = lax.rsqrt(jnp.mean(centred * centred, axis=-1, keepdims=True) + EPS)
    return centred * scale, scale


def geometry(segment):
    length = segment.shape[0]
    places = jnp.arange(length, dtype=jnp.int32)
    same_seg = segment[:, None] == segment[None, :]
    starts = jnp.min(jnp.where(same_seg, places[None, :], length), axis=1)
    prompt_len = jnp.sum((segment == 0).astype(jnp.int32))
    position = jnp.where(segment == 0, places, prompt_len + places - starts)
    allowed = (position[None, :] <= position[:, None]) & ((segment[None, :] == 0) | same_seg)
    offset = (position[:, None] - position[None, :]).astype(F32)
    return jnp.where(allowed, offset, FAR)


class Place:
    def __init__(self):
        self.s, self.zh, self.zl, self.y, self.t = (lax.axis_index(a) for a in ("s", "zh", "zl", "y", "t"))
        self.outer = lax.axis_size("zh")
        self.far = self.outer * 2

    def block(self, zh, zl, y):
        return (zh * 2 + zl) * 2 + y

    def meet(self):
        barrier = pltpu.get_barrier_semaphore()
        others = [{"t": self.t ^ 1}, {"y": self.y ^ 1}]
        others += [{"s": self.s ^ 1, "zl": self.zl ^ k} for k in range(2)]
        others += [{"zh": self.zh ^ (k // 2), "zl": self.zl ^ (k % 2)} for k in range(1, self.far)]
        for other in others:
            pl.semaphore_signal(barrier, inc=1, device_id=other, device_id_type=MESH)
        pl.semaphore_wait(barrier, len(others))


def remote(src, dst, send, recv, **where):
    return pltpu.make_async_remote_copy(
        src_ref=src, dst_ref=dst, send_sem=send, recv_sem=recv, device_id=where, device_id_type=MESH
    )


def row_loop(kinds, rows, fn):
    per = rows // CHUNK

    def step(j, carry):
        fn(j // per, pl.ds(pl.multiple_of((j % per) * CHUNK, CHUNK), CHUNK))
        return carry

    lax.fori_loop(0, kinds * per, step, 0)


class Sums:
    def __init__(self, me, part, full, tbuf, rbuf, sems):
        self.me, self.part, self.full, self.tbuf, self.rbuf, self.sems = me, part, full, tbuf, rbuf, sems
        s, zl, t = me.s, me.zl, me.t
        self.core = [
            remote(part.at[zl ^ dzl, :, s ^ ds, t ^ 1], tbuf.at[i], sems.at[0, i], sems.at[1, i], t=t ^ 1)
            for i, (ds, dzl) in enumerate(REL)
        ]
        self.sect = [
            remote(part.at[zl ^ dzl, :, s ^ 1, t], rbuf.at[i], sems.at[2, i], sems.at[3, i], s=s ^ 1)
            for i, dzl in enumerate((1, 0))
        ]
        self.pair = remote(part.at[zl ^ 1, :, s, t], rbuf.at[2], sems.at[2, 2], sems.at[3, 2], zl=zl ^ 1)

    def to_core(self, *which):
        for i in which:
            self.core[i].start()

    def merge(self, i, *extra):
        me, part, tbuf, rbuf = self.me, self.part, self.tbuf, self.rbuf
        ds, dzl = REL[i]
        a, b = me.zl ^ dzl, me.s ^ ds
        self.core[i].wait_recv()

        def add(m, r):
            v = part[a, m, b, me.t, r].astype(F32) + tbuf[i, m, r].astype(F32)
            for e in extra:
                v = v + rbuf[e, m, r].astype(F32)
            part[a, m, b, me.t, r] = v.astype(BF)

        row_loop(part.shape[1], part.shape[4], add)

    def to_section(self, i):
        self.merge(2 * i)
        self.sect[i].start()

    def to_pair(self):
        self.sect[0].wait_recv()
        self.merge(1, 0)
        self.pair.start()

    def finish(self, row_fn):
        me, part, tbuf, rbuf, full = self.me, self.part, self.tbuf, self.rbuf, self.full
        self.core[3].wait_recv()
        self.sect[1].wait_recv()
        self.pair.wait_recv()

        def add(m, r):
            v = part[me.zl, m, me.s, me.t, r].astype(F32) + tbuf[3, m, r].astype(F32)
            v = v + rbuf[1, m, r].astype(F32) + rbuf[2, m, r].astype(F32)
            full[me.zl, m, me.s, me.t, r] = row_fn(m, r, v)

        row_loop(part.shape[1], part.shape[4], add)
        for c in self.core + self.sect + [self.pair]:
            c.wait_send()

    def piece(self, ds, dzl):
        return self.full.at[self.me.zl ^ dzl, :, self.me.s ^ ds, self.me.t]

    def send(self, kind, i, piece, **where):
        c = remote(piece, piece, self.sems.at[kind, i], self.sems.at[kind + 1, i], **where)
        c.start()
        return c

    def spread(self):
        me, own = self.me, self.piece(0, 0)
        self.over_z = self.send(4, 0, own, zl=me.zl ^ 1)
        self.over_s = self.send(4, 1, own, s=me.s ^ 1)
        self.cross = [self.send(6, 0, own, t=me.t ^ 1)]

    def collect(self, between=None):
        me = self.me
        self.over_z.wait_recv()
        other = self.piece(0, 1)
        both = self.send(4, 2, other, s=me.s ^ 1)
        self.cross.append(self.send(6, 1, other, t=me.t ^ 1))
        self.over_s.wait_recv()
        self.cross.append(self.send(6, 2, self.piece(1, 0), t=me.t ^ 1))
        if between:
            between()
        both.wait_recv()
        self.cross.append(self.send(6, 3, self.piece(1, 1), t=me.t ^ 1))
        for c in self.cross:
            c.wait_recv()
        for c in self.cross + [self.over_z, self.over_s, both]:
            c.wait_send()


def sums_scratch(mb, share, width):
    return [
        pltpu.VMEM((2, mb, 2, 2, share, width), BF),
        pltpu.VMEM((4, mb, share, width), BF),
        pltpu.VMEM((3, mb, share, width), BF),
        pltpu.SemaphoreType.DMA((8, 4)),
    ]


class Staged:
    def __init__(self, src, dst, buf, sems):
        self.load = pltpu.make_async_copy(src, buf, sems.at[0])
        self.store = pltpu.make_async_copy(buf, dst, sems.at[1])

    def start(self):
        self.load.start()

    def turn(self):
        self.load.wait()
        self.store.start()

    def wait(self):
        self.store.wait()


class Fetch:
    def __init__(self, me, layer, pairs, sems, bufs):
        self.me, self.pairs, self.sems = me, pairs, sems
        self.first, self.far, self.parts, self.near = [], {}, {}, []
        home = me.block(me.zh, me.zl, me.y)
        for p, (half, whole) in enumerate(pairs):
            c = whole.shape[-1]
            src = lambda q, half=half, c=c: half.at[layer, :, :, pl.ds(pl.multiple_of(q * c, c), c)]
            dst = whole.at[:, home]
            self.first.append(Staged(src(me.zl), dst, bufs[p], sems.at[p, 4]))
            for k in range(1, me.far):
                where = {"zh": me.zh ^ (k // 2), "zl": me.zl ^ (k % 2)}
                cut = half.shape[2] // PARTS
                for q in range(PARTS):
                    r = pl.ds(q * cut, cut)
                    self.parts[p, k, q] = remote(
                        src(where["zl"]).at[:, r], dst.at[:, r], sems.at[p, 0, k], sems.at[p, 1, k], **where
                    )
                self.far[p, k] = remote(src(where["zl"]), dst, sems.at[p, 0, k], sems.at[p, 1, k], **where)
            self.near.append([remote(src(me.zl), dst, sems.at[p, 2, 0], sems.at[p, 3, 0], y=me.y ^ 1)])
        self.waves = waves(me.far)

    def start(self, *ps):
        for p in ps:
            self.near[p][0].start()
            self.first[p].start()

    def turn(self, *ps):
        for p in ps:
            self.first[p].turn()

    def send(self, p, wave, q):
        for k in self.waves[wave]:
            self.parts[p, k, q].start()

    def units(self, ps, before=None):
        for wave in range(2):
            for q in range(PARTS):
                first = wave == 0 and q == 0
                second = wave == 0 and q == 1

                def issue(wave=wave, q=q, first=first, second=second):
                    if first:
                        if before:
                            before()
                        self.start(*ps)
                    if second:
                        self.turn(*ps)
                    for p in ps:
                        self.send(p, wave, q)

                def forward(wave=wave):
                    for p in ps:
                        self.pass_on(p, wave)

                yield issue, forward if q == PARTS - 1 else None

    def pass_on(self, p, wave):
        me = self.me
        for k in self.waves[wave]:
            self.far[p, k].wait_recv()
            whole = self.pairs[p][1]
            piece = whole.at[:, me.block(me.zh ^ (k // 2), me.zl ^ (k % 2), me.y)]
            on = remote(piece, piece, self.sems.at[p, 2, k], self.sems.at[p, 3, k], y=me.y ^ 1)
            on.start()
            self.near[p].append(on)

    def ready(self, *ps):
        for p in ps:
            self.first[p].wait()
            for c in self.near[p]:
                c.wait_recv()

    def finish(self):
        for c in list(self.far.values()) + [c for near in self.near for c in near]:
            c.wait_send()


class Pump:
    def __init__(self, *units, lag=5):
        self.units = [u for group in units for u in group]
        self.issued, self.clock, self.lag, self.waiting = 0, 0, lag, []

    def step(self, n=1):
        for _ in range(n):
            self.clock += 1
            if self.issued < len(self.units):
                issue, forward = self.units[self.issued]
                issue()
                self.issued += 1
                if forward:
                    self.waiting.append((self.clock, self.issued, forward))
            while self.waiting and self.waiting[0][0] + self.lag <= self.clock:
                self.waiting.pop(0)[2]()

    def through(self, n):
        self.step(max(0, min(n, len(self.units)) - self.issued))
        while self.waiting and self.waiting[0][1] <= n:
            self.waiting.pop(0)[2]()


def fetch_scratch(shapes, far, rows):
    return [pltpu.SemaphoreType.DMA((len(shapes), 5, far))] + [pltpu.VMEM((k, rows, c), BF) for k, c in shapes]


class YSum:
    def __init__(self, me, terms, own, total, sems):
        self.me, self.own, self.total, self.terms = me, own, total, terms
        self.copies, self.loads = [], []
        for k in range(1, me.far):
            zh, zl = me.zh ^ (k // 2), me.zl ^ (k % 2)
            src = terms.at[:, me.block(zh, zl, me.y ^ 1)]
            self.copies.append((k, remote(src, total.at[:, k - 1], sems.at[0, k], sems.at[1, k], y=me.y ^ 1)))
            if own is not None:
                here = terms.at[:, me.block(zh, zl, me.y)]
                self.loads.append(pltpu.make_async_copy(here, own.at[:, k - 1], sems.at[2, k]))

    def start(self):
        for _, c in self.copies:
            c.start()
        for c in self.loads:
            c.start()

    def add(self):
        me = self.me
        for c in self.loads:
            c.wait()
        for k, c in self.copies:
            c.wait_recv()
            b = me.block(me.zh ^ (k // 2), me.zl ^ (k % 2), me.y)

            def one(m, r, k=k, b=b):
                mine = self.terms[m, b, r] if self.own is None else self.own[m, k - 1, r]
                self.total[m, k - 1, r] = (self.total[m, k - 1, r].astype(F32) + mine.astype(F32)).astype(BF)

            row_loop(self.total.shape[0], self.total.shape[2], one)

    def finish(self):
        for _, c in self.copies:
            c.wait_send()


class ZSum:
    def __init__(self, me, total, terms, got, own, near, out, sems):
        self.me, self.total, self.got, self.own, self.near, self.out = me, total, got, own, near, out
        self.copies, self.parts = {}, {}
        cut = total.shape[2] // PARTS
        for k in range(1, me.far):
            where = {"zh": me.zh ^ (k // 2), "zl": me.zl ^ (k % 2)}
            src, dst, a, b = total.at[:, k - 1], got.at[:, k - 1], sems.at[0, k], sems.at[1, k]
            self.copies[k] = remote(src, dst, a, b, **where)
            for q in range(PARTS):
                r = pl.ds(q * cut, cut)
                self.parts[k, q] = remote(src.at[:, r], dst.at[:, r], a, b, **where)
        self.load = pltpu.make_async_copy(terms.at[:, me.block(me.zh, me.zl, me.y)], own, sems.at[2, 0])
        self.home = remote(
            terms.at[:, me.block(me.zh, me.zl, me.y ^ 1)], near, sems.at[0, 0], sems.at[1, 0], y=me.y ^ 1
        )

    def start(self):
        self.load.start()
        self.home.start()

    def units(self):
        for wave in waves(self.me.far):
            for q in range(PARTS):
                yield lambda wave=wave, q=q: [self.parts[k, q].start() for k in wave], None

    def add(self):
        me, c = self.me, self.total.shape[3]
        self.load.wait()
        self.home.wait_recv()
        for copy in self.copies.values():
            copy.wait_recv()

        def one(m, r):
            same = self.own[m, r].astype(F32) + self.near[m, r].astype(F32)
            other = self.got[m, 0, r].astype(F32)
            for k in range(2, me.far):
                if k % 2:
                    other = other + self.got[m, k - 1, r].astype(F32)
                else:
                    same = same + self.got[m, k - 1, r].astype(F32)
            self.out[m, r, pl.ds(pl.multiple_of(me.zl * c, c), c)] = same.astype(BF)
            self.out[m, r, pl.ds(pl.multiple_of((me.zl ^ 1) * c, c), c)] = other.astype(BF)

        row_loop(self.total.shape[0], self.total.shape[2], one)

    def finish(self):
        for copy in self.copies.values():
            copy.wait_send()
        self.home.wait_send()


def z_scratch(k, c, far, rows):
    return [
        pltpu.VMEM((k, far - 1, rows, c), BF),
        pltpu.VMEM((k, rows, c), BF),
        pltpu.VMEM((k, rows, c), BF),
        pltpu.SemaphoreType.DMA((3, far)),
    ]


def waves(far):
    ks = range(1, far)
    return [[k for k in ks if k % 2 == 0 or k == 1], [k for k in ks if k % 2 and k > 1]]


class XMove:
    def __init__(self, me, layer, src, dst, sems):
        self.me, self.layer = me, layer
        half = src.shape[1] // 2
        self.copies = []
        for i in range(2):
            r = pl.ds(i * half, half)
            self.copies.append(remote(src.at[:, r], dst.at[:, r], sems.at[0, i], sems.at[1, i], s=me.s ^ 1))

    def start(self, i):
        @pl.when(self.me.s != self.layer)
        def _():
            self.copies[i].start()

    def finish(self):
        @pl.when(self.me.s != self.layer)
        def _():
            for c in self.copies:
                c.wait_send()

        @pl.when(self.me.s == self.layer)
        def _():
            for c in self.copies:
                c.wait_recv()


class Moves:
    def __init__(self, me, plan, chain, x_layer, ins, outs, scratch):
        ny, nz, nx = plan
        scratch = list(scratch)
        self.y = [YSum(me, ins[i], scratch[2 * i], outs[i], scratch[2 * i + 1]) for i in range(ny)]
        scratch = scratch[2 * ny :]
        zs, terms, xs = ins[ny : ny + nz], ins[ny + nz : ny + 2 * nz], ins[ny + 2 * nz :]
        self.z = []
        for i in range(nz):
            got, own, near, sems = scratch[4 * i : 4 * i + 4]
            self.z.append(ZSum(me, zs[i], terms[i], got, own, near, outs[ny + i], sems))
        scratch = scratch[4 * nz :]
        self.x = [XMove(me, x_layer, xs[i], outs[ny + nz + i], scratch[i]) for i in range(nx)]
        scratch = scratch[nx:]
        self.after = []
        for i in range(ny if chain else 0):
            got, own, near, sems = scratch[4 * i : 4 * i + 4]
            self.after.append(ZSum(me, outs[i], ins[i], got, own, near, outs[ny + nz + nx + i], sems))

        self.pump = Pump(*(c.units() for c in self.z))

    def start(self, n):
        self.step(n)
        for c in self.x:
            c.start(0)
        for c in self.y + self.z + self.after:
            c.start()

    def step(self, n=1):
        self.pump.step(n)

    def middle(self):
        for c in self.y:
            c.add()
        for group in zip(*(c.units() for c in self.after)):
            self.pump.units.append((lambda group=group: [u() for u, _ in group], None))

    def more_x(self):
        for c in self.x:
            c.start(1)

    def finish(self):
        self.pump.through(len(self.pump.units))
        for c in self.z + self.after:
            c.add()
        for c in self.y + self.z + self.x + self.after:
            c.finish()


def moves_parts(plan, chain, far, rows):
    ys, zs, xs = plan
    cs = ys if chain else ()
    specs = [AN] * len(ys) + [VM] * len(zs) + [AN] * (len(zs) + len(xs))
    outs = [((k, far - 1, rows, c), BF) for k, c in ys]
    outs += [((k, rows, 2 * c), BF) for group in (zs, xs, cs) for k, c in group]
    out_specs = [VM] * len(ys) + [VM] * len(zs) + [AN] * len(xs) + [VM] * len(cs)
    scratch = []
    for k, c in ys:
        scratch += [pltpu.VMEM((k, far - 1, rows, c), BF), pltpu.SemaphoreType.DMA((3, far))]
    for k, c in zs:
        scratch += z_scratch(k, c, far, rows)
    scratch += [pltpu.SemaphoreType.DMA((2, 2))] * len(xs)
    for k, c in cs:
        scratch += z_scratch(k, c, far, rows)
    return specs, outs, out_specs, scratch


VM = pl.BlockSpec(memory_space=pltpu.VMEM)
SM = pl.BlockSpec(memory_space=pltpu.SMEM)
AN = pl.BlockSpec(memory_space=pl.ANY)


def call(body, cid, ins, in_specs, outs, out_specs, scratch, flops=0):
    return pl.pallas_call(
        body,
        out_shape=[jax.ShapeDtypeStruct(sh, dt) for sh, dt in outs],
        in_specs=in_specs,
        out_specs=out_specs,
        scratch_shapes=scratch,
        compiler_params=pltpu.CompilerParams(
            collective_id=cid, has_side_effects=True, vmem_limit_bytes=60 * 1024 * 1024
        ),
    )(*ins)


def rows_of(ref, a, m):
    v = ref[a, m]
    return v.reshape(-1, v.shape[-1])


def put_rows(ref, a, m, v):
    ref[a, m] = v.reshape(ref.shape[2:])


def norm_rows(src, dst, a, m, gain, shift):
    share = src.shape[4]

    def one(q, r):
        vh, _ = normalize(src[a, m, q // 2, q % 2, r].astype(F32))
        dst[a, m, q // 2, q % 2, r] = (vh * gain + shift).astype(BF)

    row_loop(4, share, one)


def lanes(width):
    return lax.broadcasted_iota(jnp.int32, (1, width), 1)


def head_mask(h):
    return (lanes(2 * HEAD_DIM) // HEAD_DIM) == h


def softmax_parts(q, k, pen, slope):
    sc = dot_t(q * jnp.asarray(HEAD_DIM**-0.5, BF), k) - slope * pen
    lifted = jnp.exp(sc - jnp.max(sc, axis=-1, keepdims=True))
    return lifted * (1.0 / jnp.sum(lifted, axis=-1, keepdims=True))


def halves_of(me, mb, group, sums, hook=None):
    lax.fori_loop(0, mb, lambda m, c: (group(me.zl ^ 1, m), c)[1], 0)
    sums.to_core(0, 1)
    group(me.zl, 0)
    sums.to_section(0)
    if hook:
        hook()
    lax.fori_loop(1, mb, lambda m, c: (group(me.zl, m), c)[1], 0)
    sums.to_core(2, 3)
    sums.to_section(1)
    sums.to_pair()


def halves_apart(me, mb, group, sums, hook):
    for i in range(2 * mb):
        group((me.zl ^ 1) if i < mb else me.zl, i % mb)
        if i == mb - 1:
            sums.to_core(0, 1)
        if i == mb:
            sums.to_section(0)
        hook(i)
    sums.to_core(2, 3)
    sums.to_section(1)
    sums.to_pair()
    hook(2 * mb)


def product(dst, k, left, right, nt=256):
    rows = dst.shape[2]

    def step(j, carry):
        cols = pl.ds(pl.multiple_of(j * nt, nt), nt)
        v = row_dot(left[:, :, :, :, :, cols].reshape(-1, nt), right()).astype(BF)
        dst[k, pl.ds(j * (nt // rows), nt // rows)] = v.reshape(nt // rows, rows, v.shape[-1])
        return carry

    lax.fori_loop(0, left.shape[-1] // nt, step, 0)


def flat(ref):
    v = ref[...]
    return v.reshape(-1, v.shape[-1])


PACE = (
    (0, 1, 1, 1, 2),
    (5, 3),
    (1, 1, 1, 1),
    (1, 0, 0, 0, 2),
    (5, 3),
    (2, 2, 2, 2, 2),
    (5, 2),
)


def forward_all(
    qkv, o, up, dn, x_in, cot, own_qv, own_up, own_vecs, slopes, own_pen,
    c_all, x1, vecs, bias_up, pen, qkv_h, o_h, up_h, dn_h, wqkv0, wo0, wup0, wdn0, wqkv1, wo1, wup1, wdn1,
    normed0, proj0, mixed0, xo0, hid0, nt0, normed1, proj1, mixed1, xo1, hid1, nt1,
    part, tbuf, rbuf, sems0, sems1, sems2, xbuf, normed, two, proj, mixed, act, hidden, x_own,
    wqkv, wo, wup, wdn, wsems, stash_sems, msems, xsems, cot_stage, psems, bias, wide_up, *rest
):
    stage, packs = rest[:4], rest[4:]
    me = Place()
    me.meet()
    mb = part.shape[1]
    cq, hq = wo.shape[-1], wup.shape[-1]
    tile = 512
    quarter = me.s * 2 + me.zl

    swaps = [
        remote(src, dst.at[me.s], psems.at[0, i], psems.at[1, i], s=me.s ^ 1)
        for i, (src, dst) in enumerate(((own_vecs, vecs), (own_qv, bias), (own_up, wide_up)))
    ]
    swaps.append(remote(own_pen, pen.at[me.zl], psems.at[0, 3], psems.at[1, 3], zl=me.zl ^ 1))
    for c in swaps:
        c.start()
    vecs[me.s] = own_vecs[...]
    bias[me.s] = own_qv[...]
    wide_up[me.s] = own_up[...]
    pen[me.zl] = own_pen[...]

    jobs = []
    for p, (own, half) in enumerate(((qkv, qkv_h), (o, o_h), (up, up_h), (dn, dn_h))):
        w = own.shape[-1] // 2
        cols = lambda q, w=w: pl.ds(pl.multiple_of(q * w, w), w)
        there = remote(own.at[:, :, cols(me.s ^ 1)], half.at[me.s], msems.at[p, 0], msems.at[p, 1], s=me.s ^ 1)
        here = Staged(own.at[:, :, cols(me.s)], half.at[me.s], stage[p], msems.at[p, pl.ds(2, 2)])
        jobs.append((there, here))
    for there, _ in jobs[:2]:
        there.start()
    x_local = pltpu.make_async_copy(x_in, xbuf.at[me.zl], xsems.at[0, 4])
    x_across = remote(
        x_in.at[:, :, me.t], xbuf.at[me.zl, :, :, me.t], xsems.at[0, 0], xsems.at[0, 1], zl=me.zl ^ 1
    )
    x_piece = xbuf.at[me.zl ^ 1, :, :, me.t]
    x_cross = remote(x_piece, x_piece, xsems.at[0, 2], xsems.at[0, 3], t=me.t ^ 1)
    c_local = Staged(cot, c_all.at[me.zl], cot_stage, xsems.at[1, pl.ds(4, 2)])
    c_across = remote(cot.at[:, :, me.t], c_all.at[me.zl, :, :, me.t], xsems.at[1, 0], xsems.at[1, 1], zl=me.zl ^ 1)
    c_piece = c_all.at[me.zl ^ 1, :, :, me.t]
    c_cross = remote(c_piece, c_piece, xsems.at[1, 2], xsems.at[1, 3], t=me.t ^ 1)
    x_across.start()
    for _, here in jobs:
        here.start()
    x_local.start()
    c_local.start()
    for _, here in jobs:
        here.turn()
    c_local.turn()
    x_local.wait()

    def norm(a, layer):
        for m in range(mb):
            norm_rows(xbuf, normed, a, m, vecs[layer, 0:1], vecs[layer, 1:2])

    for c in swaps:
        c.wait()
    up_cols = pl.ds(pl.multiple_of(quarter * hq, hq), hq)
    for layer in range(2):
        bias_up[layer] = wide_up[layer, :, up_cols]
    qv_cols = pl.ds(pl.multiple_of(quarter * cq, cq), cq)
    for there, here in jobs[:2]:
        here.wait()
        there.wait_recv()
    att0 = Fetch(me, 0, ((qkv_h, wqkv0), (o_h, wo0)), packs[0], packs[1:3])
    ff0 = Fetch(me, 0, ((up_h, wup0), (dn_h, wdn0)), packs[3], packs[4:6])
    att1 = Fetch(me, 1, ((qkv_h, wqkv1), (o_h, wo1)), packs[6], packs[1:3])
    ff1 = Fetch(me, 1, ((up_h, wup1), (dn_h, wdn1)), packs[7], packs[4:6])

    def gate(*js):
        def wait():
            for j in js:
                jobs[j][1].wait()
                jobs[j][0].wait_recv()

        return wait

    per = 2 * PARTS
    pump = Pump(
        att0.units((0, 1)),
        ff0.units((0,), gate(2)),
        ff0.units((1,), gate(3)),
        att1.units((0, 1)),
        ff1.units((0,)),
        ff1.units((1,)),
    )
    pump.step(per)
    for there, _ in jobs[2:]:
        there.start()
    x_across.wait_recv()
    x_cross.start()
    norm(me.zl, 0)
    pump.waiting.pop(0)[2]()
    x_cross.wait()
    norm(me.zl ^ 1, 0)
    pump.step(per)
    pump.through(per)
    c_across.start()

    loads = {}

    def load(i, src, dst):
        loads[i] = pltpu.make_async_copy(src, dst, wsems.at[i])
        loads[i].start()

    stashes = []

    def stash(src, dst):
        c = pltpu.make_async_copy(src, dst, stash_sems.at[len(stashes)])
        c.start()
        stashes.append(c)

    def attention(layer, sums, hook):
        def group(a, m):
            if layer:
                norm_rows(xbuf, normed, a, m, vecs[layer, 0:1], vecs[layer, 1:2])
            nv = rows_of(normed, a, m)
            for k in range(3):
                v = dot(nv, flat(wqkv.at[k]))
                if k == 0:
                    v = v + bias[layer, 0:1, qv_cols]
                if k == 2:
                    v = v + bias[layer, 1:2, qv_cols]
                proj[k, a, m] = v.astype(BF)
            pv = pen[a, m].astype(F32)
            for pair in range(cq // (2 * HEAD_DIM)):
                cols = slice(pair * 2 * HEAD_DIM, (pair + 1) * 2 * HEAD_DIM)
                q, k, v = proj[0, a, m, :, cols], proj[1, a, m, :, cols], proj[2, a, m, :, cols]
                got = []
                for h in range(2):
                    probs = softmax_parts(jnp.where(head_mask(h), q, jnp.zeros_like(q)), k, pv, slopes[pair * 2 + h])
                    got.append(dot(probs.astype(BF), v))
                mixed[a, m, :, cols] = jnp.where(head_mask(0), got[0], got[1]).astype(BF)
            put_rows(part, a, m, dot_t(mixed[a, m], flat(wo)).astype(BF))

        halves_apart(me, mb, group, sums, hook)

    def attention_rows(layer):
        def rows(m, r, v):
            xr = xbuf[me.zl, m, me.s, me.t, r]
            x_own[m, r] = xr
            hid = xr.astype(F32) + v + vecs[layer, 4:5]
            hidden[m, r] = hid
            vh, _ = normalize(hid)
            return (vh * vecs[layer, 2:3] + vecs[layer, 3:4]).astype(BF)

        return rows

    sums = Sums(me, part, two, tbuf, rbuf, sems0)
    att0.ready(0, 1)
    load(0, wqkv0, wqkv)
    load(1, wo0, wo)
    loads[0].wait()
    loads[1].wait()

    def paced(*steps):
        return lambda i: pump.step(steps[i]) if i < len(steps) else None

    attention(0, sums, paced(*PACE[0]))
    stash(normed, normed0)
    stash(proj, proj0)
    stash(mixed, mixed0)
    sums.finish(attention_rows(0))
    sums.spread()
    pump.step(PACE[1][0])
    stash(hidden, hid0)
    stash(x_own, xo0)
    c_across.wait_recv()
    c_cross.start()
    sums.collect(lambda: pump.step(PACE[1][1]))
    stash(two, nt0)
    pump.through(2 * per)
    ff0.ready(0)
    load(2, wup0, wup)
    loads[2].wait()

    def up_group(a, m):
        nv = rows_of(two, a, m)
        for j in range(hq // tile):
            cols = slice(j * tile, (j + 1) * tile)
            u = dot(nv, wup[:, :, :, cols].reshape(-1, tile)) + bias_up[0, :, cols]
            act[a, m, :, cols] = (u * (0.5 + 0.5 * lax.erf(u * (0.5**0.5)))).astype(BF)

    for i in range(2 * mb):
        up_group(i // mb, i % mb)
        pump.step(PACE[2][i])
    pump.through(3 * per)
    ff0.ready(1)
    load(3, wdn0, wdn)
    loads[3].wait()
    sums = Sums(me, part, xbuf, tbuf, rbuf, sems1)
    halves_apart(
        me, mb, lambda a, m: put_rows(part, a, m, dot_t(act[a, m], flat(wdn)).astype(BF)), sums, paced(*PACE[3])
    )
    sums.finish(lambda m, r, v: (hidden[m, r] + v + vecs[0, 5:6]).astype(BF))
    sums.spread()
    pump.step(PACE[4][0])
    sums.collect(lambda: pump.step(PACE[4][1]))
    stash(xbuf.at[me.zl], x1)
    for c in stashes[:-1]:
        c.wait()
    pump.through(4 * per)
    att1.ready(0, 1)
    load(4, wqkv1, wqkv)
    load(5, wo1, wo)
    loads[4].wait()
    loads[5].wait()

    sums = Sums(me, part, two, tbuf, rbuf, sems2)

    attention(1, sums, paced(*PACE[5]))
    n_done = len(stashes) - 1
    stash(normed, normed1)
    stash(proj, proj1)
    stash(mixed, mixed1)
    sums.finish(attention_rows(1))
    sums.spread()
    pump.step(PACE[6][0])
    stash(hidden, hid1)
    stash(x_own, xo1)
    sums.collect(lambda: pump.step(PACE[6][1]))
    stash(two, nt1)
    pump.through(6 * per)
    ff1.ready(0, 1)
    for c in (att0, ff0, att1, ff1):
        c.finish()
    for c in stashes[n_done:]:
        c.wait()
    for there, _ in jobs:
        there.wait_send()
    x_across.wait_send()
    c_local.wait()
    c_across.wait_send()
    c_cross.wait()


def ln_back(e, v, gain):
    vh, r = normalize(v)
    f = e * gain
    grad = r * (f - jnp.mean(f, -1, keepdims=True) - vh * jnp.mean(f * vh, -1, keepdims=True))
    return grad, e * vh


def fold(v):
    return v[:8] + v[8:]


PACE_FF = (3, (1, 1, 1, 1, 1), 2, 4, 2, 2)
PACE_ATT = ((3, (0, 1, 1, 0, 2), 0, 2), (3, (1, 1, 1, 1, 1), 2, 4, 2))


def ff_backward(layer, plan, g, normed_two, wup, wdn, vecs, hidden, bias, *rest):
    rest = list(rest)
    vecs, bias = vecs.at[layer], bias.at[layer]
    chain = bool(plan[0])
    n_in, n_out = sum(plan) + plan[1], sum(plan) + (plan[0] if chain else 0)
    ins, rest = rest[:n_in], rest[n_in:]
    g_up_out, g_dn_out, act_out, grad_hidden, small, small_up, full, dn_sum = rest[:8]
    outs, rest = rest[8 : 8 + n_out], rest[8 + n_out :]
    part, tbuf, rbuf, sems, gu, ysems, g_up, g_dn, act, osems = rest[:10]
    writes = [
        pltpu.make_async_copy(a, b, osems.at[i])
        for i, (a, b) in enumerate(((act, act_out), (g_dn, g_dn_out), (g_up, g_up_out)))
    ]
    me = Place()
    me.meet()
    moves = Moves(me, plan, chain, layer + 1, ins, outs, rest[10:])
    moves.start(PACE_FF[0])
    sums = Sums(me, part, full, tbuf, rbuf, sems)
    mb = g.shape[1]
    hq = wup.shape[-1]
    tile = 512
    small[...] = jnp.zeros_like(small)
    small_up[...] = jnp.zeros_like(small_up)

    def group(a, m):
        gv = rows_of(g, a, m)
        nv = rows_of(normed_two, a, m)
        for j in range(hq // tile):
            cols = slice(j * tile, (j + 1) * tile)
            u = dot(nv, wup[:, cols]) + bias[:, cols]
            cdf = 0.5 + 0.5 * lax.erf(u * (0.5**0.5))
            act[a, m, :, cols] = (u * cdf).astype(BF)
            slope = cdf + u * (jnp.exp(-0.5 * u * u) * 0.3989422804014327)
            v = (dot(gv, wdn[:, cols]) * slope).astype(BF)
            gu[a, m, :, cols] = v
            small_up[:, cols] += jnp.sum(v.astype(F32).reshape(-1, 8, tile), axis=0)
        put_rows(part, a, m, dot_t(gu[a, m], wup[...]).astype(BF))

    halves_apart(me, mb, group, sums, lambda i: moves.step(PACE_FF[1][i]))
    product(g_dn, 0, g, lambda: flat(act))
    for c in writes[:2]:
        c.start()
    down = YSum(me, g_dn, None, dn_sum, ysems)
    down.start()
    moves.middle()
    moves.step(PACE_FF[2])

    def rows(m, r, e):
        grad, ev = ln_back(e, hidden[m, r], vecs[2:3])
        go = g[me.zl, m, me.s, me.t, r].astype(F32)
        grad = go + grad
        grad_hidden[m, r] = grad
        small[0] += fold(ev)
        small[1] += fold(e)
        small[2] += fold(grad)
        small[3] += fold(go)
        return grad.astype(BF)

    sums.finish(rows)
    sums.spread()
    moves.step(PACE_FF[3])
    moves.more_x()
    product(g_up, 0, normed_two, lambda: flat(gu))
    writes[2].start()
    moves.step(PACE_FF[4])
    sums.collect(lambda: moves.step(PACE_FF[5]))
    moves.finish()
    down.add()
    down.finish()
    for c in writes:
        c.wait()


class LocalSpread:
    def __init__(self, me, layer, full, sems):
        self.me, self.layer = me, layer
        here, there = full.at[:, me.s, me.t], full.at[:, me.s ^ 1, me.t]
        self.across = remote(here, here, sems.at[0, 0], sems.at[1, 0], s=me.s ^ 1)
        self.crosses = [
            remote(piece, piece, sems.at[0, i + 1], sems.at[1, i + 1], t=me.t ^ 1)
            for i, piece in enumerate((here, there))
        ]

    def start(self):
        @pl.when(self.me.s != self.layer)
        def _():
            self.across.start()

        self.crosses[0].start()

    def finish(self):
        @pl.when(self.me.s == self.layer)
        def _():
            self.across.wait_recv()
            self.crosses[1].start()
            self.crosses[1].wait()

        self.crosses[0].wait()

        @pl.when(self.me.s != self.layer)
        def _():
            self.across.wait_send()


class Rows:
    def __init__(self, me, ref):
        self.me, self.ref = me, ref

    def __setitem__(self, idx, value):
        _, m, s, t, r = idx
        self.ref[m, s, t, r] = value


def att_backward(layer, last, plan, gb, x_own, normed_in, proj, mixed_in, wqkv, wo, vecs, slopes, pen, grad_hidden, *rest):
    vecs = vecs.at[layer]
    rest = list(rest)
    n_in, n_out = sum(plan) + plan[1], sum(plan) + (plan[0] if last else 0)
    ins, rest = rest[:n_in], rest[n_in:]
    g_qkv_out, g_o_out, small, small_p, full = rest[:5]
    outs, rest = rest[5 : 5 + n_out], rest[5 + n_out :]
    if last:
        x_dn0, tot_qkv, tot_o = rest[:3]
        rest = rest[3:]
    part, tbuf, rbuf, sems, gp, lsems, dsems, ysems, normed, mixed, g_qkv, g_o, osems = rest[:13]
    reads = [pltpu.make_async_copy(normed_in, normed, osems.at[0]), pltpu.make_async_copy(mixed_in, mixed, osems.at[1])]
    writes = [pltpu.make_async_copy(g_o, g_o_out, osems.at[2]), pltpu.make_async_copy(g_qkv, g_qkv_out, osems.at[3])]
    for c in reads:
        c.start()
    me = Place()
    me.meet()
    moves = Moves(me, plan, last, layer + 1, ins, outs, rest[13:])
    pace = PACE_ATT[1 if last else 0]
    moves.start(pace[0])
    if last:
        early = XMove(me, layer, moves.z[0].out, x_dn0, dsems)
    sums = Sums(me, part, Rows(me, full) if last else full, tbuf, rbuf, sems)
    mb = gb.shape[1]
    cq = wo.shape[-1]
    small[...] = jnp.zeros_like(small)
    small_p[...] = jnp.zeros_like(small_p)
    scale = float(HEAD_DIM) ** -0.5

    def group(a, m):
        gm_all = dot(rows_of(gb, a, m), wo[...]).astype(BF)
        pv = pen[a, m].astype(F32)
        for pair in range(cq // (2 * HEAD_DIM)):
            cols = slice(pair * 2 * HEAD_DIM, (pair + 1) * 2 * HEAD_DIM)
            q, k, v = proj[0, a, m, :, cols], proj[1, a, m, :, cols], proj[2, a, m, :, cols]
            gm = gm_all[:, cols]
            gq, gk, gv = [], [], []
            for h in range(2):
                zero = jnp.zeros_like(q)
                probs = softmax_parts(jnp.where(head_mask(h), q, zero), k, pv, slopes[pair * 2 + h])
                gpr = dot_t(jnp.where(head_mask(h), gm, zero), v)
                gv.append(row_dot(probs.astype(BF), gm))
                pg = probs * gpr
                gs = (pg - probs * jnp.sum(pg, axis=-1, keepdims=True)).astype(BF)
                gq.append(dot(gs, k))
                gk.append(row_dot(gs, q))
            for i, (both, f) in enumerate(((gq, scale), (gk, scale), (gv, 1.0))):
                out = (jnp.where(head_mask(0), both[0], both[1]) * f).astype(BF)
                gp[i, a, m, :, cols] = out
                small_p[i, :, cols] += jnp.sum(out.astype(F32).reshape(-1, 8, 2 * HEAD_DIM), axis=0)
        total = dot_t(gp[0, a, m], wqkv[0]) + dot_t(gp[1, a, m], wqkv[1]) + dot_t(gp[2, a, m], wqkv[2])
        put_rows(part, a, m, total.astype(BF))

    halves_apart(me, mb, group, sums, lambda i: moves.step(pace[1][i]))
    for c in reads:
        c.wait()
    product(g_o, 0, gb, lambda: mixed[...].reshape(-1, cq))
    writes[0].start()

    def rows(m, r, e):
        grad, ev = ln_back(e, x_own[m, r].astype(F32), vecs[0:1])
        small[0] += fold(ev)
        small[1] += fold(e)
        return (grad_hidden[m, r] + grad).astype(BF)

    def qkv_products():
        for k in range(3):
            product(g_qkv, k, normed, lambda k=k: gp[k].reshape(-1, cq))
        writes[1].start()

    if last:
        moves.middle()
        moves.step(pace[2])
        qkv_products()
        here = [YSum(me, g_qkv, None, tot_qkv, ysems.at[0]), YSum(me, g_o, None, tot_o, ysems.at[1])]
        for c in here:
            c.start()
        sums.finish(rows)
        local = LocalSpread(me, layer, full, lsems)
        local.start()
        moves.step(pace[3])
        moves.more_x()
        moves.z[0].add()
        early.start(0)
        early.start(1)
        local.finish()
        moves.step(pace[4])
        for c in here:
            c.add()
        moves.z[0].finish()
        moves.z = moves.z[1:]
        moves.finish()
        for c in here:
            c.finish()
        early.finish()
    else:
        sums.finish(rows)
        sums.spread()
        moves.step(pace[3])
        moves.middle()
        qkv_products()
        sums.collect()
        moves.finish()
    for c in writes:
        c.wait()


def last_sums(
    log_outer, act, wdn, hidden, vecs, sf0, su0, sa0, sp0, sf1, su1, sa1, sp1, t_qkv, t_o, g_qkv, g_o, h_up0,
    x_up0, h_qkv0, h_o0, x_qkv0, x_o0, sec, total,
    part, tbuf, rbuf, sems, lsems, xsems, heap, hsems, *zbufs
):
    me = Place()
    me.meet()
    zs = [
        ZSum(me, a, b, *zbufs[4 * i : 4 * i + 3], c, zbufs[4 * i + 3])
        for i, (a, b, c) in enumerate(((t_qkv, g_qkv, h_qkv0), (t_o, g_o, h_o0)))
    ]
    pump = Pump([(lambda group=group: [u() for u, _ in group], None) for group in zip(*(z.units() for z in zs))])
    pump.step(2)
    for z in zs:
        z.start()
    xs = [
        XMove(me, 0, a, b, xsems.at[i])
        for i, (a, b) in enumerate(((h_up0, x_up0), (h_qkv0, x_qkv0), (h_o0, x_o0)))
    ]
    xs[0].start(0)
    mb = act.shape[1]
    sums = Sums(me, part, Rows(me, sec), tbuf, rbuf, sems)

    def group(a, m):
        put_rows(part, a, m, dot_t(act[a, m], wdn[...]).astype(BF))

    width, cq, hq = total.shape[1], sp0.shape[-1], su0.shape[-1]
    place = me.t * 4 + me.s * 2 + me.zl
    total[...] = jnp.zeros_like(total)
    for layer, (sf, su, sa, sp) in enumerate(((sf0, su0, sa0, sp0), (sf1, su1, sa1, sp1))):
        base = layer * (total.shape[0] // 2)
        for i, v in enumerate((sa[0], sf[0], sa[1], sf[1], sf[2], sf[3])):
            total[base + i : base + i + 1] = jnp.sum(v, axis=0, keepdims=True)
        for i, j in enumerate((0, 2)):
            cols = pl.ds(pl.multiple_of(place * cq, cq), cq)
            total[base + 6 + i : base + 7 + i, cols] = jnp.sum(sp[j], axis=0, keepdims=True)
        for i in range(8 * hq // width):

            @pl.when(place // (width // hq) == i)
            def _(i=i, base=base, su=su):
                cols = pl.ds(pl.multiple_of((place % (width // hq)) * hq, hq), hq)
                total[base + 8 + i : base + 9 + i, cols] = jnp.sum(su[...], axis=0, keepdims=True)

    peers = [{"t": me.t ^ 1}, {"y": me.y ^ 1}, {"s": me.s ^ 1}, {"zl": me.zl ^ 1}]
    peers += [{"zh": me.zh ^ (1 << b)} for b in range(log_outer)]

    def butterfly(lo, hi):
        for i in range(lo, min(hi, len(peers))):
            c = remote(total, heap.at[i], hsems.at[0, i], hsems.at[1, i], **peers[i])
            c.start()
            c.wait()
            total[...] += heap[i]

    halves_of(me, mb, group, sums)
    pump.step(2)
    xs[0].start(1)
    butterfly(0, 2)
    pump.step(4)
    sums.finish(lambda m, r, v: (hidden[m, r] + v + vecs[1, 5:6]).astype(BF))
    local = LocalSpread(me, 1, sec, lsems)
    local.start()
    butterfly(2, 3)
    for z, x in zip(zs, xs[1:]):
        z.add()
        x.start(0)
        x.start(1)
    local.finish()
    butterfly(3, 99)
    for c in zs + xs:
        c.finish()


def pick(v, index, dim):
    return lax.dynamic_index_in_dim(v, index, dim, keepdims=False)


def shards(x_in, cotangent, layout, w_qkv, b_qv, w_out, w_fc1, b_fc1, w_fc2, gains, biases):
    s, zl, t = (lax.axis_index(a) for a in ("s", "zl", "t"))
    outer = lax.axis_size("zh")
    far, nb = outer * 2, outer * 4
    log_outer = outer.bit_length() - 1
    mb, rows_mb, width = x_in.shape
    wrows = w_out.shape[1]
    block = w_out.shape[2]
    hid = w_fc1.shape[2]
    cq, hq = block // 4, hid // 4
    share = rows_mb // 4
    tokens = (2, mb, 2, 2, share, width)

    quarter = s * 2 + zl
    own_vecs = jnp.concatenate([jnp.stack([gains[0, 0], biases[0, 0], gains[0, 1], biases[0, 1]]), biases[0, 2:]])
    own_pen = jax.vmap(geometry)(layout.reshape(mb, rows_mb)).astype(BF)
    local_heads = cq // HEAD_DIM
    head_ids = t * (block // HEAD_DIM) + quarter * local_heads + jnp.arange(local_heads, dtype=jnp.int32)
    slopes = jnp.exp2(-8.0 * (head_ids + 1).astype(F32) / HEADS)

    own_shape = (mb, 2, 2, share, width)
    qk, oo, ff = (3, cq), (1, cq), (1, hq)
    att_w = [((3, nb, wrows, cq), BF), ((1, nb, wrows, cq), BF)]
    ff_w = [((1, nb, wrows, hq), BF)] * 2
    own_rows = (mb, share, width)
    hidden_shape = (2, mb, rows_mb, hq)
    proj_shape = (3, 2, mb, rows_mb, cq)
    mixed_shape = (2, mb, rows_mb, cq)
    act_scratch = sums_scratch(mb, share, width)
    halves = [((2, k, wrows, 2 * c), BF) for k, c in (qk, oo, ff, ff)]
    stash_outs = [
        (tokens, BF),
        (proj_shape, BF),
        (mixed_shape, BF),
        (own_rows, BF),
        (own_rows, F32),
        (tokens, BF),
    ]
    outs = [(tokens, BF), (own_shape, BF)]
    outs += [((2, 6, width), F32), ((2, 1, hq), F32), ((2, mb, GROUP, GROUP), BF)]
    outs += halves + (att_w + ff_w) * 2 + stash_outs * 2
    sem = pltpu.SemaphoreType.DMA
    cot, x1, vecs, bias_up, pen, _, _, _, _, wqkv0, wo0, wup0, wdn0, wqkv1, wo1, wup1, wdn1, *stashed = call(
        forward_all,
        0,
        (
            w_qkv[0].transpose(1, 0, 2),
            w_out,
            w_fc1,
            w_fc2,
            x_in.reshape(own_shape),
            cotangent.reshape(own_shape),
            b_qv[0],
            b_fc1,
            own_vecs,
            slopes,
            own_pen,
        ),
        [AN] * 6 + [VM] * 3 + [SM, VM],
        outs,
        [AN] * 2 + [VM] * 3 + [AN] * (len(outs) - 5),
        act_scratch
        + [sem((8, 4))] * 2
        + [pltpu.VMEM(tokens, BF)] * 3
        + [pltpu.VMEM(sh, BF) for sh in (proj_shape, mixed_shape, hidden_shape)]
        + [pltpu.VMEM(own_rows, F32), pltpu.VMEM(own_rows, BF)]
        + [pltpu.VMEM(sh, dt) for sh, dt in att_w + ff_w]
        + [sem((6,)), sem((13,)), sem((4, 4)), sem((2, 6)), pltpu.VMEM(own_shape, BF)]
        + [sem((2, 4)), pltpu.VMEM((2, 2, block), F32), pltpu.VMEM((2, 1, hid), F32)]
        + [pltpu.VMEM((k, wrows, 2 * c), BF) for k, c in (qk, oo, ff, ff)]
        + fetch_scratch((qk, oo), far, wrows)
        + fetch_scratch((ff, ff), far, wrows)
        + [sem((2, 5, far))] * 2,
    )
    normed0, proj0, mixed0, xo0, hidden0, nt0, normed1, proj1, mixed1, xo1, hidden1, nt1 = stashed
    wup0, wdn0, wup1, wdn1 = (w.reshape(width, hq) for w in (wup0, wdn0, wup1, wdn1))

    def ff_bwd(layer, cid, ins, plan, arrays):
        m_specs, m_outs, m_out_specs, m_scratch = moves_parts(plan, bool(plan[0]), far, wrows)
        outs = [
            ((1, nb, wrows, hq), BF),
            ((1, nb, wrows, hq), BF),
            (hidden_shape, BF),
            (own_rows, F32),
            ((4, 8, width), F32),
            ((8, hq), F32),
            (tokens, BF),
            ((1, far - 1, wrows, hq), BF),
        ]
        scratch = act_scratch + [
            pltpu.VMEM(hidden_shape, BF),
            pltpu.SemaphoreType.DMA((3, far)),
            pltpu.VMEM((1, nb, wrows, hq), BF),
            pltpu.VMEM((1, nb, wrows, hq), BF),
            pltpu.VMEM(hidden_shape, BF),
            sem((3,)),
        ]
        return call(
            functools.partial(ff_backward, layer, tuple(len(p) for p in plan)),
            cid,
            list(ins) + list(arrays),
            [VM] * len(ins) + m_specs,
            outs + m_outs,
            [AN] * 3 + [VM] * (len(outs) - 3) + m_out_specs,
            scratch + m_scratch,
        )

    def att_bwd(layer, cid, ins, plan, arrays):
        last = layer == 0
        m_specs, m_outs, m_out_specs, m_scratch = moves_parts(plan, last, far, wrows)
        outs = att_w + [((2, 8, width), F32), ((3, 8, cq), F32), (own_shape if last else tokens, BF)]
        scratch = act_scratch + [pltpu.VMEM(proj_shape, BF), sem((2, 3)), sem((2, 2)), sem((2, 3, far))]
        scratch += [pltpu.VMEM(sh, dt) for sh, dt in [(tokens, BF), (mixed_shape, BF)] + att_w] + [sem((4,))]
        return call(
            functools.partial(att_backward, layer, last, tuple(len(p) for p in plan)),
            cid,
            list(ins) + list(arrays),
            [VM, VM, AN, VM, AN] + [VM] * 3 + [SM, VM, VM] + m_specs,
            outs + m_outs + ([((1, wrows, 2 * hq), BF)] + [((k, far - 1, wrows, c), BF) for k, c in (qk, oo)]) * last,
            [AN, AN] + [VM] * (len(outs) - 2) + m_out_specs + [AN, VM, VM] * last,
            scratch + m_scratch,
        )

    wqkv0, wo0 = wqkv0.reshape(3, width, cq), wo0.reshape(width, cq)
    wqkv1, wo1 = wqkv1.reshape(3, width, cq), wo1.reshape(width, cq)
    g_up1, g_dn1, act1, gh1, sf1, su1, gb1, dn1_total = ff_bwd(
        1, 4, (cot, nt1, wup1, wdn1, vecs, hidden1, bias_up), ((), (), ()), ()
    )
    g_qkv1, g_o1, sa1, sp1, g0, up1_total, h_dn1 = att_bwd(
        1,
        5,
        (gb1, xo1, normed1, proj1, mixed1, wqkv1, wo1, vecs, slopes, pen, gh1),
        ((ff,), (ff,), ()),
        (g_up1, dn1_total, g_dn1),
    )
    g_up0, g_dn0, _, gh0, sf0, su0, gb0, dn0_total, _, _, h_up1, x_dn1, h_qkv1, h_o1 = ff_bwd(
        0,
        6,
        (g0, nt0, wup0, wdn0, vecs, hidden0, bias_up),
        ((qk, oo), (ff,), (ff,)),
        (g_qkv1, g_o1, up1_total, g_up1, h_dn1),
    )
    g_qkv0, g_o0, sa0, sp0, gin, _, h_dn0, x_up1, x_qkv1, x_o1, h_up0, x_dn0, qkv0_total, o0_total = att_bwd(
        0,
        7,
        (gb0, xo0, normed0, proj0, mixed0, wqkv0, wo0, vecs, slopes, pen, gh0),
        ((ff,), (ff,), (ff, qk, oo)),
        (g_up0, dn0_total, g_dn0, h_up1, h_qkv1, h_o1),
    )

    n_small = 2 * (6 + (16 * cq + 8 * hq) // width)

    def half(k, c):
        return ((k, wrows, 2 * c), BF)

    x_up0, h_qkv0, h_o0, x_qkv0, x_o0, sec1, total = call(
        functools.partial(last_sums, log_outer),
        8,
        (act1, wdn1, hidden1, vecs, sf0, su0, sa0, sp0, sf1, su1, sa1, sp1)
        + (qkv0_total, o0_total, g_qkv0, g_o0, h_up0),
        [VM] * 14 + [AN] * 3,
        [half(*ff), half(*qk), half(*oo), half(*qk), half(*oo)] + [(own_shape, BF), ((n_small, width), F32)],
        [AN] + [VM] * 2 + [AN] * 2 + [VM] * 2,
        act_scratch
        + [sem((2, 3)), sem((3, 2, 2)), pltpu.VMEM((4 + log_outer, n_small, width), F32), sem((2, 4 + log_outer))]
        + z_scratch(*qk, far, wrows)
        + z_scratch(*oo, far, wrows),
    )

    def home(own0, got0, own1, got1):
        left = jnp.where(s == 0, own0, got1)
        right = jnp.where(s == 0, got0, own1)
        return jnp.concatenate([left, right], axis=-1).astype(F32)

    g_qkv = home(h_qkv0, x_qkv0, h_qkv1, x_qkv1).transpose(1, 0, 2)[None]
    g_out = home(h_o0, x_o0, h_o1, x_o1)
    g_fc1 = home(h_up0, x_up0, h_up1, x_up1)
    g_fc2 = home(h_dn0, x_dn0, h_dn1, x_dn1)

    def of_layer(first, second):
        return jnp.where(s == 0, first.reshape(mb, rows_mb, width), second.reshape(mb, rows_mb, width))[None]

    section_outputs = of_layer(x1, sec1)
    input_grads = of_layer(gin, pick(g0, zl, 0))
    total = pick(total.reshape(2, n_small // 2, width), s, 0)
    n_qv = 16 * cq // width
    grad_gains = total[:2][None]
    grad_biases = total[2:6][None]
    grad_b_qv = pick(total[6 : 6 + n_qv].reshape(1, 2, 2, 4 * cq), t, 2)
    grad_b_fc1 = pick(total[6 + n_qv :].reshape(1, 2, 4 * hq), t, 1)
    return section_outputs, input_grads, g_qkv, grad_b_qv, g_out, g_fc1, grad_b_fc1, g_fc2, grad_gains, grad_biases


def solution(mesh):
    n_s, n_dp, n_t = mesh.shape["section"], mesh.shape["dp"], mesh.shape["tensor"]
    fine = Mesh(mesh.devices.reshape(n_s, n_dp // 4, 2, 2, n_t), ("s", "zh", "zl", "y", "t"))
    return jax.shard_map(
        shards,
        mesh=fine,
        in_specs=(
            P(None, DP, None),
            P(None, DP, None),
            P(None, DP),
            P("s", DP, None, "t"),
            P("s", None, "t"),
            P("s", DP, "t"),
            P("s", DP, "t"),
            P("s", "t"),
            P("s", DP, "t"),
            P("s", None, None),
            P("s", None, None),
        ),
        out_specs=(
            P("s", None, DP, None),
            P("s", None, DP, None),
            P("s", DP, None, "t"),
            P("s", None, "t"),
            P("s", DP, "t"),
            P("s", DP, "t"),
            P("s", "t"),
            P("s", DP, "t"),
            P("s", None, None),
            P("s", None, None),
        ),
        check_vma=False,
    )
```

```python
import functools

import jax
import jax.numpy as jnp
from jax import lax
from jax.experimental import pallas as pl
from jax.experimental.pallas import tpu as pltpu
from jax.sharding import Mesh, PartitionSpec as P

HEADS = 32
HEAD_DIM = 64
GROUP = 256
EPS = 1e-05
BF = jnp.bfloat16
F32 = jnp.float32
DP = ("zh", "zl", "y")
MESH = pl.DeviceIdType.MESH
REL = ((1, 1), (0, 1), (1, 0), (0, 0))
CHUNK = 16
PARTS = 4
FAR = 1e30


def dot(a, b):
    return jnp.dot(a, b, preferred_element_type=F32)


def dot_t(a, b):
    return lax.dot_general(a, b, (((1,), (1,)), ((), ())), preferred_element_type=F32)


def row_dot(a, b):
    return lax.dot_general(a, b, (((0,), (0,)), ((), ())), preferred_element_type=F32)


def normalize(v):
    centred = v - jnp.mean(v, axis=-1, keepdims=True)
    scale = lax.rsqrt(jnp.mean(centred * centred, axis=-1, keepdims=True) + EPS)
    return centred * scale, scale


def geometry(segment):
    length = segment.shape[0]
    places = jnp.arange(length, dtype=jnp.int32)
    same_seg = segment[:, None] == segment[None, :]
    starts = jnp.min(jnp.where(same_seg, places[None, :], length), axis=1)
    prompt_len = jnp.sum((segment == 0).astype(jnp.int32))
    position = jnp.where(segment == 0, places, prompt_len + places - starts)
    allowed = (position[None, :] <= position[:, None]) & ((segment[None, :] == 0) | same_seg)
    offset = (position[:, None] - position[None, :]).astype(F32)
    return jnp.where(allowed, offset, FAR)


class Place:
    def __init__(self):
        self.s, self.zh, self.zl, self.y, self.t = (lax.axis_index(a) for a in ("s", "zh", "zl", "y", "t"))
        self.outer = lax.axis_size("zh")
        self.far = self.outer * 2

    def block(self, zh, zl, y):
        return (zh * 2 + zl) * 2 + y

    def meet(self):
        barrier = pltpu.get_barrier_semaphore()
        others = [{"t": self.t ^ 1}, {"y": self.y ^ 1}]
        others += [{"s": self.s ^ 1, "zl": self.zl ^ k} for k in range(2)]
        others += [{"zh": self.zh ^ (k // 2), "zl": self.zl ^ (k % 2)} for k in range(1, self.far)]
        for other in others:
            pl.semaphore_signal(barrier, inc=1, device_id=other, device_id_type=MESH)
        pl.semaphore_wait(barrier, len(others))


def remote(src, dst, send, recv, **where):
    return pltpu.make_async_remote_copy(
        src_ref=src, dst_ref=dst, send_sem=send, recv_sem=recv, device_id=where, device_id_type=MESH
    )


def row_loop(kinds, rows, fn):
    per = rows // CHUNK

    def step(j, carry):
        fn(j // per, pl.ds(pl.multiple_of((j % per) * CHUNK, CHUNK), CHUNK))
        return carry

    lax.fori_loop(0, kinds * per, step, 0)


class Sums:
    def __init__(self, me, part, full, tbuf, rbuf, sems):
        self.me, self.part, self.full, self.tbuf, self.rbuf, self.sems = me, part, full, tbuf, rbuf, sems
        s, zl, t = me.s, me.zl, me.t
        self.core = [
            remote(part.at[zl ^ dzl, :, s ^ ds, t ^ 1], tbuf.at[i], sems.at[0, i], sems.at[1, i], t=t ^ 1)
            for i, (ds, dzl) in enumerate(REL)
        ]
        self.sect = [
            remote(part.at[zl ^ dzl, :, s ^ 1, t], rbuf.at[i], sems.at[2, i], sems.at[3, i], s=s ^ 1)
            for i, dzl in enumerate((1, 0))
        ]
        self.pair = remote(part.at[zl ^ 1, :, s, t], rbuf.at[2], sems.at[2, 2], sems.at[3, 2], zl=zl ^ 1)

    def to_core(self, *which):
        for i in which:
            self.core[i].start()

    def merge(self, i, *extra):
        me, part, tbuf, rbuf = self.me, self.part, self.tbuf, self.rbuf
        ds, dzl = REL[i]
        a, b = me.zl ^ dzl, me.s ^ ds
        self.core[i].wait_recv()

        def add(m, r):
            v = part[a, m, b, me.t, r].astype(F32) + tbuf[i, m, r].astype(F32)
            for e in extra:
                v = v + rbuf[e, m, r].astype(F32)
            part[a, m, b, me.t, r] = v.astype(BF)

        row_loop(part.shape[1], part.shape[4], add)

    def to_section(self, i):
        self.merge(2 * i)
        self.sect[i].start()

    def to_pair(self):
        self.sect[0].wait_recv()
        self.merge(1, 0)
        self.pair.start()

    def finish(self, row_fn):
        me, part, tbuf, rbuf, full = self.me, self.part, self.tbuf, self.rbuf, self.full
        self.core[3].wait_recv()
        self.sect[1].wait_recv()
        self.pair.wait_recv()

        def add(m, r):
            v = part[me.zl, m, me.s, me.t, r].astype(F32) + tbuf[3, m, r].astype(F32)
            v = v + rbuf[1, m, r].astype(F32) + rbuf[2, m, r].astype(F32)
            full[me.zl, m, me.s, me.t, r] = row_fn(m, r, v)

        row_loop(part.shape[1], part.shape[4], add)
        for c in self.core + self.sect + [self.pair]:
            c.wait_send()

    def piece(self, ds, dzl):
        return self.full.at[self.me.zl ^ dzl, :, self.me.s ^ ds, self.me.t]

    def send(self, kind, i, piece, **where):
        c = remote(piece, piece, self.sems.at[kind, i], self.sems.at[kind + 1, i], **where)
        c.start()
        return c

    def spread(self):
        me, own = self.me, self.piece(0, 0)
        self.over_z = self.send(4, 0, own, zl=me.zl ^ 1)
        self.over_s = self.send(4, 1, own, s=me.s ^ 1)
        self.cross = [self.send(6, 0, own, t=me.t ^ 1)]

    def collect(self, between=None):
        me = self.me
        self.over_z.wait_recv()
        other = self.piece(0, 1)
        both = self.send(4, 2, other, s=me.s ^ 1)
        self.cross.append(self.send(6, 1, other, t=me.t ^ 1))
        self.over_s.wait_recv()
        self.cross.append(self.send(6, 2, self.piece(1, 0), t=me.t ^ 1))
        if between:
            between()
        both.wait_recv()
        self.cross.append(self.send(6, 3, self.piece(1, 1), t=me.t ^ 1))
        for c in self.cross:
            c.wait_recv()
        for c in self.cross + [self.over_z, self.over_s, both]:
            c.wait_send()


def sums_scratch(mb, share, width):
    return [
        pltpu.VMEM((2, mb, 2, 2, share, width), BF),
        pltpu.VMEM((4, mb, share, width), BF),
        pltpu.VMEM((3, mb, share, width), BF),
        pltpu.SemaphoreType.DMA((8, 4)),
    ]


class Staged:
    def __init__(self, src, dst, buf, sems):
        self.load = pltpu.make_async_copy(src, buf, sems.at[0])
        self.store = pltpu.make_async_copy(buf, dst, sems.at[1])

    def start(self):
        self.load.start()

    def turn(self):
        self.load.wait()
        self.store.start()

    def wait(self):
        self.store.wait()


class Fetch:
    def __init__(self, me, layer, pairs, sems, bufs):
        self.me, self.pairs, self.sems = me, pairs, sems
        self.first, self.far, self.parts, self.near = [], {}, {}, []
        home = me.block(me.zh, me.zl, me.y)
        for p, (half, whole) in enumerate(pairs):
            c = whole.shape[-1]
            src = lambda q, half=half, c=c: half.at[layer, :, :, pl.ds(pl.multiple_of(q * c, c), c)]
            dst = whole.at[:, home]
            self.first.append(Staged(src(me.zl), dst, bufs[p], sems.at[p, 4]))
            for k in range(1, me.far):
                where = {"zh": me.zh ^ (k // 2), "zl": me.zl ^ (k % 2)}
                cut = half.shape[2] // PARTS
                for q in range(PARTS):
                    r = pl.ds(q * cut, cut)
                    self.parts[p, k, q] = remote(
                        src(where["zl"]).at[:, r], dst.at[:, r], sems.at[p, 0, k], sems.at[p, 1, k], **where
                    )
                self.far[p, k] = remote(src(where["zl"]), dst, sems.at[p, 0, k], sems.at[p, 1, k], **where)
            self.near.append([remote(src(me.zl), dst, sems.at[p, 2, 0], sems.at[p, 3, 0], y=me.y ^ 1)])
        self.waves = waves(me.far)

    def start(self, *ps):
        for p in ps:
            self.near[p][0].start()
            self.first[p].start()

    def turn(self, *ps):
        for p in ps:
            self.first[p].turn()

    def send(self, p, wave, q):
        for k in self.waves[wave]:
            self.parts[p, k, q].start()

    def units(self, ps, before=None):
        for wave in range(2):
            for q in range(PARTS):
                first = wave == 0 and q == 0
                second = wave == 0 and q == 1

                def issue(wave=wave, q=q, first=first, second=second):
                    if first:
                        if before:
                            before()
                        self.start(*ps)
                    if second:
                        self.turn(*ps)
                    for p in ps:
                        self.send(p, wave, q)

                def forward(wave=wave):
                    for p in ps:
                        self.pass_on(p, wave)

                yield issue, forward if q == PARTS - 1 else None

    def pass_on(self, p, wave):
        me = self.me
        for k in self.waves[wave]:
            self.far[p, k].wait_recv()
            whole = self.pairs[p][1]
            piece = whole.at[:, me.block(me.zh ^ (k // 2), me.zl ^ (k % 2), me.y)]
            on = remote(piece, piece, self.sems.at[p, 2, k], self.sems.at[p, 3, k], y=me.y ^ 1)
            on.start()
            self.near[p].append(on)

    def ready(self, *ps):
        for p in ps:
            self.first[p].wait()
            for c in self.near[p]:
                c.wait_recv()

    def finish(self):
        for c in list(self.far.values()) + [c for near in self.near for c in near]:
            c.wait_send()


class Pump:
    def __init__(self, *units, lag=5):
        self.units = [u for group in units for u in group]
        self.issued, self.clock, self.lag, self.waiting = 0, 0, lag, []

    def step(self, n=1):
        for _ in range(n):
            self.clock += 1
            if self.issued < len(self.units):
                issue, forward = self.units[self.issued]
                issue()
                self.issued += 1
                if forward:
                    self.waiting.append((self.clock, self.issued, forward))
            while self.waiting and self.waiting[0][0] + self.lag <= self.clock:
                self.waiting.pop(0)[2]()

    def through(self, n):
        self.step(max(0, min(n, len(self.units)) - self.issued))
        while self.waiting and self.waiting[0][1] <= n:
            self.waiting.pop(0)[2]()


def fetch_scratch(shapes, far, rows):
    return [pltpu.SemaphoreType.DMA((len(shapes), 5, far))] + [pltpu.VMEM((k, rows, c), BF) for k, c in shapes]


class YSum:
    def __init__(self, me, terms, own, total, sems):
        self.me, self.own, self.total, self.terms = me, own, total, terms
        self.copies, self.loads = [], []
        for k in range(1, me.far):
            zh, zl = me.zh ^ (k // 2), me.zl ^ (k % 2)
            src = terms.at[:, me.block(zh, zl, me.y ^ 1)]
            self.copies.append((k, remote(src, total.at[:, k - 1], sems.at[0, k], sems.at[1, k], y=me.y ^ 1)))
            if own is not None:
                here = terms.at[:, me.block(zh, zl, me.y)]
                self.loads.append(pltpu.make_async_copy(here, own.at[:, k - 1], sems.at[2, k]))

    def start(self):
        for _, c in self.copies:
            c.start()
        for c in self.loads:
            c.start()

    def add(self):
        me = self.me
        for c in self.loads:
            c.wait()
        for k, c in self.copies:
            c.wait_recv()
            b = me.block(me.zh ^ (k // 2), me.zl ^ (k % 2), me.y)

            def one(m, r, k=k, b=b):
                mine = self.terms[m, b, r] if self.own is None else self.own[m, k - 1, r]
                self.total[m, k - 1, r] = (self.total[m, k - 1, r].astype(F32) + mine.astype(F32)).astype(BF)

            row_loop(self.total.shape[0], self.total.shape[2], one)

    def finish(self):
        for _, c in self.copies:
            c.wait_send()


class ZSum:
    def __init__(self, me, total, terms, got, own, near, out, sems):
        self.me, self.total, self.got, self.own, self.near, self.out = me, total, got, own, near, out
        self.copies, self.parts = {}, {}
        cut = total.shape[2] // PARTS
        for k in range(1, me.far):
            where = {"zh": me.zh ^ (k // 2), "zl": me.zl ^ (k % 2)}
            src, dst, a, b = total.at[:, k - 1], got.at[:, k - 1], sems.at[0, k], sems.at[1, k]
            self.copies[k] = remote(src, dst, a, b, **where)
            for q in range(PARTS):
                r = pl.ds(q * cut, cut)
                self.parts[k, q] = remote(src.at[:, r], dst.at[:, r], a, b, **where)
        self.load = pltpu.make_async_copy(terms.at[:, me.block(me.zh, me.zl, me.y)], own, sems.at[2, 0])
        self.home = remote(
            terms.at[:, me.block(me.zh, me.zl, me.y ^ 1)], near, sems.at[0, 0], sems.at[1, 0], y=me.y ^ 1
        )

    def start(self):
        self.load.start()
        self.home.start()

    def units(self):
        for wave in waves(self.me.far):
            for q in range(PARTS):
                yield lambda wave=wave, q=q: [self.parts[k, q].start() for k in wave], None

    def add(self):
        me, c = self.me, self.total.shape[3]
        self.load.wait()
        self.home.wait_recv()
        for copy in self.copies.values():
            copy.wait_recv()

        def one(m, r):
            same = self.own[m, r].astype(F32) + self.near[m, r].astype(F32)
            other = self.got[m, 0, r].astype(F32)
            for k in range(2, me.far):
                if k % 2:
                    other = other + self.got[m, k - 1, r].astype(F32)
                else:
                    same = same + self.got[m, k - 1, r].astype(F32)
            self.out[m, r, pl.ds(pl.multiple_of(me.zl * c, c), c)] = same.astype(BF)
            self.out[m, r, pl.ds(pl.multiple_of((me.zl ^ 1) * c, c), c)] = other.astype(BF)

        row_loop(self.total.shape[0], self.total.shape[2], one)

    def finish(self):
        for copy in self.copies.values():
            copy.wait_send()
        self.home.wait_send()


def z_scratch(k, c, far, rows):
    return [
        pltpu.VMEM((k, far - 1, rows, c), BF),
        pltpu.VMEM((k, rows, c), BF),
        pltpu.VMEM((k, rows, c), BF),
        pltpu.SemaphoreType.DMA((3, far)),
    ]


def waves(far):
    ks = range(1, far)
    return [[k for k in ks if k % 2 == 0 or k == 1], [k for k in ks if k % 2 and k > 1]]


class XMove:
    def __init__(self, me, layer, src, dst, sems):
        self.me, self.layer = me, layer
        half = src.shape[1] // 2
        self.copies = []
        for i in range(2):
            r = pl.ds(i * half, half)
            self.copies.append(remote(src.at[:, r], dst.at[:, r], sems.at[0, i], sems.at[1, i], s=me.s ^ 1))

    def start(self, i):
        @pl.when(self.me.s != self.layer)
        def _():
            self.copies[i].start()

    def finish(self):
        @pl.when(self.me.s != self.layer)
        def _():
            for c in self.copies:
                c.wait_send()

        @pl.when(self.me.s == self.layer)
        def _():
            for c in self.copies:
                c.wait_recv()


class Moves:
    def __init__(self, me, plan, chain, x_layer, ins, outs, scratch):
        ny, nz, nx = plan
        scratch = list(scratch)
        self.y = [YSum(me, ins[i], scratch[2 * i], outs[i], scratch[2 * i + 1]) for i in range(ny)]
        scratch = scratch[2 * ny :]
        zs, terms, xs = ins[ny : ny + nz], ins[ny + nz : ny + 2 * nz], ins[ny + 2 * nz :]
        self.z = []
        for i in range(nz):
            got, own, near, sems = scratch[4 * i : 4 * i + 4]
            self.z.append(ZSum(me, zs[i], terms[i], got, own, near, outs[ny + i], sems))
        scratch = scratch[4 * nz :]
        self.x = [XMove(me, x_layer, xs[i], outs[ny + nz + i], scratch[i]) for i in range(nx)]
        scratch = scratch[nx:]
        self.after = []
        for i in range(ny if chain else 0):
            got, own, near, sems = scratch[4 * i : 4 * i + 4]
            self.after.append(ZSum(me, outs[i], ins[i], got, own, near, outs[ny + nz + nx + i], sems))

        self.pump = Pump(*(c.units() for c in self.z))

    def start(self, n):
        self.step(n)
        for c in self.x:
            c.start(0)
        for c in self.y + self.z + self.after:
            c.start()

    def step(self, n=1):
        self.pump.step(n)

    def middle(self):
        for c in self.y:
            c.add()
        for group in zip(*(c.units() for c in self.after)):
            self.pump.units.append((lambda group=group: [u() for u, _ in group], None))

    def more_x(self):
        for c in self.x:
            c.start(1)

    def finish(self):
        self.pump.through(len(self.pump.units))
        for c in self.z + self.after:
            c.add()
        for c in self.y + self.z + self.x + self.after:
            c.finish()


def moves_parts(plan, chain, far, rows):
    ys, zs, xs = plan
    cs = ys if chain else ()
    specs = [AN] * len(ys) + [VM] * len(zs) + [AN] * (len(zs) + len(xs))
    outs = [((k, far - 1, rows, c), BF) for k, c in ys]
    outs += [((k, rows, 2 * c), BF) for group in (zs, xs, cs) for k, c in group]
    out_specs = [VM] * len(ys) + [VM] * len(zs) + [AN] * len(xs) + [VM] * len(cs)
    scratch = []
    for k, c in ys:
        scratch += [pltpu.VMEM((k, far - 1, rows, c), BF), pltpu.SemaphoreType.DMA((3, far))]
    for k, c in zs:
        scratch += z_scratch(k, c, far, rows)
    scratch += [pltpu.SemaphoreType.DMA((2, 2))] * len(xs)
    for k, c in cs:
        scratch += z_scratch(k, c, far, rows)
    return specs, outs, out_specs, scratch


VM = pl.BlockSpec(memory_space=pltpu.VMEM)
SM = pl.BlockSpec(memory_space=pltpu.SMEM)
AN = pl.BlockSpec(memory_space=pl.ANY)


def call(body, cid, ins, in_specs, outs, out_specs, scratch, flops=0):
    return pl.pallas_call(
        body,
        out_shape=[jax.ShapeDtypeStruct(sh, dt) for sh, dt in outs],
        in_specs=in_specs,
        out_specs=out_specs,
        scratch_shapes=scratch,
        compiler_params=pltpu.CompilerParams(
            collective_id=cid, has_side_effects=True, vmem_limit_bytes=60 * 1024 * 1024
        ),
    )(*ins)


def rows_of(ref, a, m):
    v = ref[a, m]
    return v.reshape(-1, v.shape[-1])


def put_rows(ref, a, m, v):
    ref[a, m] = v.reshape(ref.shape[2:])


def norm_rows(src, dst, a, m, gain, shift):
    share = src.shape[4]

    def one(q, r):
        vh, _ = normalize(src[a, m, q // 2, q % 2, r].astype(F32))
        dst[a, m, q // 2, q % 2, r] = (vh * gain + shift).astype(BF)

    row_loop(4, share, one)


def lanes(width):
    return lax.broadcasted_iota(jnp.int32, (1, width), 1)


def head_mask(h):
    return (lanes(2 * HEAD_DIM) // HEAD_DIM) == h


def softmax_parts(q, k, pen, slope):
    sc = dot_t(q * jnp.asarray(HEAD_DIM**-0.5, BF), k) - slope * pen
    lifted = jnp.exp(sc - jnp.max(sc, axis=-1, keepdims=True))
    return lifted * (1.0 / jnp.sum(lifted, axis=-1, keepdims=True))


def halves_of(me, mb, group, sums, hook=None):
    lax.fori_loop(0, mb, lambda m, c: (group(me.zl ^ 1, m), c)[1], 0)
    sums.to_core(0, 1)
    group(me.zl, 0)
    sums.to_section(0)
    if hook:
        hook()
    lax.fori_loop(1, mb, lambda m, c: (group(me.zl, m), c)[1], 0)
    sums.to_core(2, 3)
    sums.to_section(1)
    sums.to_pair()


def halves_apart(me, mb, group, sums, hook):
    for i in range(2 * mb):
        group((me.zl ^ 1) if i < mb else me.zl, i % mb)
        if i == mb - 1:
            sums.to_core(0, 1)
        if i == mb:
            sums.to_section(0)
        hook(i)
    sums.to_core(2, 3)
    sums.to_section(1)
    sums.to_pair()
    hook(2 * mb)


def product(dst, k, left, right, nt=256):
    rows = dst.shape[2]

    def step(j, carry):
        cols = pl.ds(pl.multiple_of(j * nt, nt), nt)
        v = row_dot(left[:, :, :, :, :, cols].reshape(-1, nt), right()).astype(BF)
        dst[k, pl.ds(j * (nt // rows), nt // rows)] = v.reshape(nt // rows, rows, v.shape[-1])
        return carry

    lax.fori_loop(0, left.shape[-1] // nt, step, 0)


def flat(ref):
    v = ref[...]
    return v.reshape(-1, v.shape[-1])


PACE = (
    (0, 1, 1, 1, 2),
    (5, 3),
    (1, 1, 1, 1),
    (1, 0, 0, 0, 2),
    (5, 3),
    (2, 2, 2, 2, 2),
    (5, 2),
)


def forward_all(
    qkv, o, up, dn, x_in, cot, own_qv, own_up, own_vecs, slopes, own_pen,
    c_all, x1, vecs, bias_up, pen, qkv_h, o_h, up_h, dn_h, wqkv0, wo0, wup0, wdn0, wqkv1, wo1, wup1, wdn1,
    normed0, proj0, mixed0, xo0, hid0, nt0, normed1, proj1, mixed1, xo1, hid1, nt1,
    part, tbuf, rbuf, sems0, sems1, sems2, xbuf, normed, two, proj, mixed, act, hidden, x_own,
    wqkv, wo, wup, wdn, wsems, stash_sems, msems, xsems, cot_stage, psems, bias, wide_up, *rest
):
    stage, packs = rest[:4], rest[4:]
    me = Place()
    me.meet()
    mb = part.shape[1]
    cq, hq = wo.shape[-1], wup.shape[-1]
    tile = 512
    quarter = me.s * 2 + me.zl

    swaps = [
        remote(src, dst.at[me.s], psems.at[0, i], psems.at[1, i], s=me.s ^ 1)
        for i, (src, dst) in enumerate(((own_vecs, vecs), (own_qv, bias), (own_up, wide_up)))
    ]
    swaps.append(remote(own_pen, pen.at[me.zl], psems.at[0, 3], psems.at[1, 3], zl=me.zl ^ 1))
    for c in swaps:
        c.start()
    vecs[me.s] = own_vecs[...]
    bias[me.s] = own_qv[...]
    wide_up[me.s] = own_up[...]
    pen[me.zl] = own_pen[...]

    jobs = []
    for p, (own, half) in enumerate(((qkv, qkv_h), (o, o_h), (up, up_h), (dn, dn_h))):
        w = own.shape[-1] // 2
        cols = lambda q, w=w: pl.ds(pl.multiple_of(q * w, w), w)
        there = remote(own.at[:, :, cols(me.s ^ 1)], half.at[me.s], msems.at[p, 0], msems.at[p, 1], s=me.s ^ 1)
        here = Staged(own.at[:, :, cols(me.s)], half.at[me.s], stage[p], msems.at[p, pl.ds(2, 2)])
        jobs.append((there, here))
    for there, _ in jobs[:2]:
        there.start()
    x_local = pltpu.make_async_copy(x_in, xbuf.at[me.zl], xsems.at[0, 4])
    x_across = remote(
        x_in.at[:, :, me.t], xbuf.at[me.zl, :, :, me.t], xsems.at[0, 0], xsems.at[0, 1], zl=me.zl ^ 1
    )
    x_piece = xbuf.at[me.zl ^ 1, :, :, me.t]
    x_cross = remote(x_piece, x_piece, xsems.at[0, 2], xsems.at[0, 3], t=me.t ^ 1)
    c_local = Staged(cot, c_all.at[me.zl], cot_stage, xsems.at[1, pl.ds(4, 2)])
    c_across = remote(cot.at[:, :, me.t], c_all.at[me.zl, :, :, me.t], xsems.at[1, 0], xsems.at[1, 1], zl=me.zl ^ 1)
    c_piece = c_all.at[me.zl ^ 1, :, :, me.t]
    c_cross = remote(c_piece, c_piece, xsems.at[1, 2], xsems.at[1, 3], t=me.t ^ 1)
    x_across.start()
    for _, here in jobs:
        here.start()
    x_local.start()
    c_local.start()
    for _, here in jobs:
        here.turn()
    c_local.turn()
    x_local.wait()

    def norm(a, layer):
        for m in range(mb):
            norm_rows(xbuf, normed, a, m, vecs[layer, 0:1], vecs[layer, 1:2])

    for c in swaps:
        c.wait()
    up_cols = pl.ds(pl.multiple_of(quarter * hq, hq), hq)
    for layer in range(2):
        bias_up[layer] = wide_up[layer, :, up_cols]
    qv_cols = pl.ds(pl.multiple_of(quarter * cq, cq), cq)
    for there, here in jobs[:2]:
        here.wait()
        there.wait_recv()
    att0 = Fetch(me, 0, ((qkv_h, wqkv0), (o_h, wo0)), packs[0], packs[1:3])
    ff0 = Fetch(me, 0, ((up_h, wup0), (dn_h, wdn0)), packs[3], packs[4:6])
    att1 = Fetch(me, 1, ((qkv_h, wqkv1), (o_h, wo1)), packs[6], packs[1:3])
    ff1 = Fetch(me, 1, ((up_h, wup1), (dn_h, wdn1)), packs[7], packs[4:6])

    def gate(*js):
        def wait():
            for j in js:
                jobs[j][1].wait()
                jobs[j][0].wait_recv()

        return wait

    per = 2 * PARTS
    pump = Pump(
        att0.units((0, 1)),
        ff0.units((0,), gate(2)),
        ff0.units((1,), gate(3)),
        att1.units((0, 1)),
        ff1.units((0,)),
        ff1.units((1,)),
    )
    pump.step(per)
    for there, _ in jobs[2:]:
        there.start()
    x_across.wait_recv()
    x_cross.start()
    norm(me.zl, 0)
    pump.waiting.pop(0)[2]()
    x_cross.wait()
    norm(me.zl ^ 1, 0)
    pump.step(per)
    pump.through(per)
    c_across.start()

    loads = {}

    def load(i, src, dst):
        loads[i] = pltpu.make_async_copy(src, dst, wsems.at[i])
        loads[i].start()

    stashes = []

    def stash(src, dst):
        c = pltpu.make_async_copy(src, dst, stash_sems.at[len(stashes)])
        c.start()
        stashes.append(c)

    def attention(layer, sums, hook):
        def group(a, m):
            if layer:
                norm_rows(xbuf, normed, a, m, vecs[layer, 0:1], vecs[layer, 1:2])
            nv = rows_of(normed, a, m)
            for k in range(3):
                v = dot(nv, flat(wqkv.at[k]))
                if k == 0:
                    v = v + bias[layer, 0:1, qv_cols]
                if k == 2:
                    v = v + bias[layer, 1:2, qv_cols]
                proj[k, a, m] = v.astype(BF)
            pv = pen[a, m].astype(F32)
            for pair in range(cq // (2 * HEAD_DIM)):
                cols = slice(pair * 2 * HEAD_DIM, (pair + 1) * 2 * HEAD_DIM)
                q, k, v = proj[0, a, m, :, cols], proj[1, a, m, :, cols], proj[2, a, m, :, cols]
                got = []
                for h in range(2):
                    probs = softmax_parts(jnp.where(head_mask(h), q, jnp.zeros_like(q)), k, pv, slopes[pair * 2 + h])
                    got.append(dot(probs.astype(BF), v))
                mixed[a, m, :, cols] = jnp.where(head_mask(0), got[0], got[1]).astype(BF)
            put_rows(part, a, m, dot_t(mixed[a, m], flat(wo)).astype(BF))

        halves_apart(me, mb, group, sums, hook)

    def attention_rows(layer):
        def rows(m, r, v):
            xr = xbuf[me.zl, m, me.s, me.t, r]
            x_own[m, r] = xr
            hid = xr.astype(F32) + v + vecs[layer, 4:5]
            hidden[m, r] = hid
            vh, _ = normalize(hid)
            return (vh * vecs[layer, 2:3] + vecs[layer, 3:4]).astype(BF)

        return rows

    sums = Sums(me, part, two, tbuf, rbuf, sems0)
    att0.ready(0, 1)
    load(0, wqkv0, wqkv)
    load(1, wo0, wo)
    loads[0].wait()
    loads[1].wait()

    def paced(*steps):
        return lambda i: pump.step(steps[i]) if i < len(steps) else None

    attention(0, sums, paced(*PACE[0]))
    stash(normed, normed0)
    stash(proj, proj0)
    stash(mixed, mixed0)
    sums.finish(attention_rows(0))
    sums.spread()
    pump.step(PACE[1][0])
    stash(hidden, hid0)
    stash(x_own, xo0)
    c_across.wait_recv()
    c_cross.start()
    sums.collect(lambda: pump.step(PACE[1][1]))
    stash(two, nt0)
    pump.through(2 * per)
    ff0.ready(0)
    load(2, wup0, wup)
    loads[2].wait()

    def up_group(a, m):
        nv = rows_of(two, a, m)
        for j in range(hq // tile):
            cols = slice(j * tile, (j + 1) * tile)
            u = dot(nv, wup[:, :, :, cols].reshape(-1, tile)) + bias_up[0, :, cols]
            act[a, m, :, cols] = (u * (0.5 + 0.5 * lax.erf(u * (0.5**0.5)))).astype(BF)

    for i in range(2 * mb):
        up_group(i // mb, i % mb)
        pump.step(PACE[2][i])
    pump.through(3 * per)
    ff0.ready(1)
    load(3, wdn0, wdn)
    loads[3].wait()
    sums = Sums(me, part, xbuf, tbuf, rbuf, sems1)
    halves_apart(
        me, mb, lambda a, m: put_rows(part, a, m, dot_t(act[a, m], flat(wdn)).astype(BF)), sums, paced(*PACE[3])
    )
    sums.finish(lambda m, r, v: (hidden[m, r] + v + vecs[0, 5:6]).astype(BF))
    sums.spread()
    pump.step(PACE[4][0])
    sums.collect(lambda: pump.step(PACE[4][1]))
    stash(xbuf.at[me.zl], x1)
    for c in stashes[:-1]:
        c.wait()
    pump.through(4 * per)
    att1.ready(0, 1)
    load(4, wqkv1, wqkv)
    load(5, wo1, wo)
    loads[4].wait()
    loads[5].wait()

    sums = Sums(me, part, two, tbuf, rbuf, sems2)

    attention(1, sums, paced(*PACE[5]))
    n_done = len(stashes) - 1
    stash(normed, normed1)
    stash(proj, proj1)
    stash(mixed, mixed1)
    sums.finish(attention_rows(1))
    sums.spread()
    pump.step(PACE[6][0])
    stash(hidden, hid1)
    stash(x_own, xo1)
    sums.collect(lambda: pump.step(PACE[6][1]))
    stash(two, nt1)
    pump.through(6 * per)
    ff1.ready(0, 1)
    for c in (att0, ff0, att1, ff1):
        c.finish()
    for c in stashes[n_done:]:
        c.wait()
    for there, _ in jobs:
        there.wait_send()
    x_across.wait_send()
    c_local.wait()
    c_across.wait_send()
    c_cross.wait()


def ln_back(e, v, gain):
    vh, r = normalize(v)
    f = e * gain
    grad = r * (f - jnp.mean(f, -1, keepdims=True) - vh * jnp.mean(f * vh, -1, keepdims=True))
    return grad, e * vh


def fold(v):
    return v[:8] + v[8:]


PACE_FF = (3, (1, 1, 1, 1, 1), 2, 4, 2, 2)
PACE_ATT = ((3, (0, 1, 1, 0, 2), 0, 2), (3, (1, 1, 1, 1, 1), 2, 4, 2))


def ff_backward(layer, plan, g_in, nt_in, wup_in, wdn_in, vecs, hidden, bias, *rest):
    rest = list(rest)
    vecs, bias = vecs.at[layer], bias.at[layer]
    chain = bool(plan[0])
    n_in, n_out = sum(plan) + plan[1], sum(plan) + (plan[0] if chain else 0)
    ins, rest = rest[:n_in], rest[n_in:]
    g_up_out, g_dn_out, act_out, grad_hidden, small, small_up, full, dn_sum = rest[:8]
    outs, rest = rest[8 : 8 + n_out], rest[8 + n_out :]
    part, tbuf, rbuf, sems, gu, ysems, g_up, g_dn, act, osems, g, normed_two, wup, wdn, isems = rest[:15]
    reads = [
        pltpu.make_async_copy(a, b, isems.at[i])
        for i, (a, b) in enumerate(((g_in, g), (nt_in, normed_two), (wup_in, wup), (wdn_in, wdn)))
    ]
    for c in reads:
        c.start()
    writes = [
        pltpu.make_async_copy(a, b, osems.at[i])
        for i, (a, b) in enumerate(((act, act_out), (g_dn, g_dn_out), (g_up, g_up_out)))
    ]
    me = Place()
    me.meet()
    moves = Moves(me, plan, chain, layer + 1, ins, outs, rest[15:])
    moves.start(PACE_FF[0])
    for c in reads:
        c.wait()
    sums = Sums(me, part, full, tbuf, rbuf, sems)
    mb = g.shape[1]
    hq = wup.shape[-1]
    tile = 512
    small[...] = jnp.zeros_like(small)
    small_up[...] = jnp.zeros_like(small_up)

    def group(a, m):
        gv = rows_of(g, a, m)
        nv = rows_of(normed_two, a, m)
        for j in range(hq // tile):
            cols = slice(j * tile, (j + 1) * tile)
            u = dot(nv, wup[:, cols]) + bias[:, cols]
            cdf = 0.5 + 0.5 * lax.erf(u * (0.5**0.5))
            act[a, m, :, cols] = (u * cdf).astype(BF)
            slope = cdf + u * (jnp.exp(-0.5 * u * u) * 0.3989422804014327)
            v = (dot(gv, wdn[:, cols]) * slope).astype(BF)
            gu[a, m, :, cols] = v
            small_up[:, cols] += jnp.sum(v.astype(F32).reshape(-1, 8, tile), axis=0)
        put_rows(part, a, m, dot_t(gu[a, m], wup[...]).astype(BF))

    halves_apart(me, mb, group, sums, lambda i: moves.step(PACE_FF[1][i]))
    product(g_dn, 0, g, lambda: flat(act))
    for c in writes[:2]:
        c.start()
    down = YSum(me, g_dn, None, dn_sum, ysems)
    down.start()
    moves.middle()
    moves.step(PACE_FF[2])

    def rows(m, r, e):
        grad, ev = ln_back(e, hidden[m, r], vecs[2:3])
        go = g[me.zl, m, me.s, me.t, r].astype(F32)
        grad = go + grad
        grad_hidden[m, r] = grad
        small[0] += fold(ev)
        small[1] += fold(e)
        small[2] += fold(grad)
        small[3] += fold(go)
        return grad.astype(BF)

    sums.finish(rows)
    sums.spread()
    moves.step(PACE_FF[3])
    moves.more_x()
    product(g_up, 0, normed_two, lambda: flat(gu))
    writes[2].start()
    moves.step(PACE_FF[4])
    sums.collect(lambda: moves.step(PACE_FF[5]))
    moves.finish()
    down.add()
    down.finish()
    for c in writes:
        c.wait()


class LocalSpread:
    def __init__(self, me, layer, full, sems):
        self.me, self.layer = me, layer
        here, there = full.at[:, me.s, me.t], full.at[:, me.s ^ 1, me.t]
        self.across = remote(here, here, sems.at[0, 0], sems.at[1, 0], s=me.s ^ 1)
        self.crosses = [
            remote(piece, piece, sems.at[0, i + 1], sems.at[1, i + 1], t=me.t ^ 1)
            for i, piece in enumerate((here, there))
        ]

    def start(self):
        @pl.when(self.me.s != self.layer)
        def _():
            self.across.start()

        self.crosses[0].start()

    def finish(self):
        @pl.when(self.me.s == self.layer)
        def _():
            self.across.wait_recv()
            self.crosses[1].start()
            self.crosses[1].wait()

        self.crosses[0].wait()

        @pl.when(self.me.s != self.layer)
        def _():
            self.across.wait_send()


class Rows:
    def __init__(self, me, ref):
        self.me, self.ref = me, ref

    def __setitem__(self, idx, value):
        _, m, s, t, r = idx
        self.ref[m, s, t, r] = value


def att_backward(layer, last, plan, gb, x_own, normed_in, proj, mixed_in, wqkv, wo, vecs, slopes, pen, grad_hidden, *rest):
    vecs = vecs.at[layer]
    rest = list(rest)
    n_in, n_out = sum(plan) + plan[1], sum(plan) + (plan[0] if last else 0)
    ins, rest = rest[:n_in], rest[n_in:]
    g_qkv_out, g_o_out, small, small_p, full = rest[:5]
    outs, rest = rest[5 : 5 + n_out], rest[5 + n_out :]
    if last:
        x_dn0, tot_qkv, tot_o = rest[:3]
        rest = rest[3:]
    part, tbuf, rbuf, sems, gp, lsems, dsems, ysems, normed, mixed, g_qkv, g_o, osems = rest[:13]
    reads = [pltpu.make_async_copy(normed_in, normed, osems.at[0]), pltpu.make_async_copy(mixed_in, mixed, osems.at[1])]
    writes = [pltpu.make_async_copy(g_o, g_o_out, osems.at[2]), pltpu.make_async_copy(g_qkv, g_qkv_out, osems.at[3])]
    for c in reads:
        c.start()
    me = Place()
    me.meet()
    moves = Moves(me, plan, last, layer + 1, ins, outs, rest[13:])
    pace = PACE_ATT[1 if last else 0]
    moves.start(pace[0])
    if last:
        early = XMove(me, layer, moves.z[0].out, x_dn0, dsems)
    sums = Sums(me, part, Rows(me, full) if last else full, tbuf, rbuf, sems)
    mb = gb.shape[1]
    cq = wo.shape[-1]
    small[...] = jnp.zeros_like(small)
    small_p[...] = jnp.zeros_like(small_p)
    scale = float(HEAD_DIM) ** -0.5

    def group(a, m):
        gm_all = dot(rows_of(gb, a, m), wo[...]).astype(BF)
        pv = pen[a, m].astype(F32)
        for pair in range(cq // (2 * HEAD_DIM)):
            cols = slice(pair * 2 * HEAD_DIM, (pair + 1) * 2 * HEAD_DIM)
            q, k, v = proj[0, a, m, :, cols], proj[1, a, m, :, cols], proj[2, a, m, :, cols]
            gm = gm_all[:, cols]
            gq, gk, gv = [], [], []
            for h in range(2):
                zero = jnp.zeros_like(q)
                probs = softmax_parts(jnp.where(head_mask(h), q, zero), k, pv, slopes[pair * 2 + h])
                gpr = dot_t(jnp.where(head_mask(h), gm, zero), v)
                gv.append(row_dot(probs.astype(BF), gm))
                pg = probs * gpr
                gs = (pg - probs * jnp.sum(pg, axis=-1, keepdims=True)).astype(BF)
                gq.append(dot(gs, k))
                gk.append(row_dot(gs, q))
            for i, (both, f) in enumerate(((gq, scale), (gk, scale), (gv, 1.0))):
                out = (jnp.where(head_mask(0), both[0], both[1]) * f).astype(BF)
                gp[i, a, m, :, cols] = out
                small_p[i, :, cols] += jnp.sum(out.astype(F32).reshape(-1, 8, 2 * HEAD_DIM), axis=0)
        total = dot_t(gp[0, a, m], wqkv[0]) + dot_t(gp[1, a, m], wqkv[1]) + dot_t(gp[2, a, m], wqkv[2])
        put_rows(part, a, m, total.astype(BF))

    halves_apart(me, mb, group, sums, lambda i: moves.step(pace[1][i]))
    for c in reads:
        c.wait()
    product(g_o, 0, gb, lambda: mixed[...].reshape(-1, cq))
    writes[0].start()

    def rows(m, r, e):
        grad, ev = ln_back(e, x_own[m, r].astype(F32), vecs[0:1])
        small[0] += fold(ev)
        small[1] += fold(e)
        return (grad_hidden[m, r] + grad).astype(BF)

    def qkv_products():
        for k in range(3):
            product(g_qkv, k, normed, lambda k=k: gp[k].reshape(-1, cq))
        writes[1].start()

    if last:
        moves.middle()
        moves.step(pace[2])
        qkv_products()
        here = [YSum(me, g_qkv, None, tot_qkv, ysems.at[0]), YSum(me, g_o, None, tot_o, ysems.at[1])]
        for c in here:
            c.start()
        sums.finish(rows)
        local = LocalSpread(me, layer, full, lsems)
        local.start()
        moves.step(pace[3])
        moves.more_x()
        moves.z[0].add()
        early.start(0)
        early.start(1)
        local.finish()
        moves.step(pace[4])
        for c in here:
            c.add()
        moves.z[0].finish()
        moves.z = moves.z[1:]
        moves.finish()
        for c in here:
            c.finish()
        early.finish()
    else:
        sums.finish(rows)
        sums.spread()
        moves.step(pace[3])
        moves.middle()
        qkv_products()
        sums.collect()
        moves.finish()
    for c in writes:
        c.wait()


def last_sums(
    log_outer, act_in, wdn_in, hidden, vecs, sf0, su0, sa0, sp0, sf1, su1, sa1, sp1, t_qkv, t_o, g_qkv, g_o, h_up0,
    x_up0, h_qkv0, h_o0, x_qkv0, x_o0, sec, total,
    part, tbuf, rbuf, sems, lsems, xsems, heap, hsems, act, wdn, isems, *zbufs
):
    reads = [pltpu.make_async_copy(act_in, act, isems.at[0]), pltpu.make_async_copy(wdn_in, wdn, isems.at[1])]
    for c in reads:
        c.start()
    me = Place()
    me.meet()
    zs = [
        ZSum(me, a, b, *zbufs[4 * i : 4 * i + 3], c, zbufs[4 * i + 3])
        for i, (a, b, c) in enumerate(((t_qkv, g_qkv, h_qkv0), (t_o, g_o, h_o0)))
    ]
    pump = Pump([(lambda group=group: [u() for u, _ in group], None) for group in zip(*(z.units() for z in zs))])
    pump.step(2)
    for z in zs:
        z.start()
    xs = [
        XMove(me, 0, a, b, xsems.at[i])
        for i, (a, b) in enumerate(((h_up0, x_up0), (h_qkv0, x_qkv0), (h_o0, x_o0)))
    ]
    xs[0].start(0)
    mb = act.shape[1]
    sums = Sums(me, part, Rows(me, sec), tbuf, rbuf, sems)

    def group(a, m):
        put_rows(part, a, m, dot_t(act[a, m], wdn[...]).astype(BF))

    width, cq, hq = total.shape[1], sp0.shape[-1], su0.shape[-1]
    place = me.t * 4 + me.s * 2 + me.zl
    total[...] = jnp.zeros_like(total)
    for layer, (sf, su, sa, sp) in enumerate(((sf0, su0, sa0, sp0), (sf1, su1, sa1, sp1))):
        base = layer * (total.shape[0] // 2)
        for i, v in enumerate((sa[0], sf[0], sa[1], sf[1], sf[2], sf[3])):
            total[base + i : base + i + 1] = jnp.sum(v, axis=0, keepdims=True)
        for i, j in enumerate((0, 2)):
            cols = pl.ds(pl.multiple_of(place * cq, cq), cq)
            total[base + 6 + i : base + 7 + i, cols] = jnp.sum(sp[j], axis=0, keepdims=True)
        for i in range(8 * hq // width):

            @pl.when(place // (width // hq) == i)
            def _(i=i, base=base, su=su):
                cols = pl.ds(pl.multiple_of((place % (width // hq)) * hq, hq), hq)
                total[base + 8 + i : base + 9 + i, cols] = jnp.sum(su[...], axis=0, keepdims=True)

    peers = [{"t": me.t ^ 1}, {"y": me.y ^ 1}, {"s": me.s ^ 1}, {"zl": me.zl ^ 1}]
    peers += [{"zh": me.zh ^ (1 << b)} for b in range(log_outer)]

    def butterfly(lo, hi):
        for i in range(lo, min(hi, len(peers))):
            c = remote(total, heap.at[i], hsems.at[0, i], hsems.at[1, i], **peers[i])
            c.start()
            c.wait()
            total[...] += heap[i]

    for c in reads:
        c.wait()
    halves_of(me, mb, group, sums)
    pump.step(2)
    xs[0].start(1)
    butterfly(0, 2)
    pump.step(4)
    sums.finish(lambda m, r, v: (hidden[m, r] + v + vecs[1, 5:6]).astype(BF))
    local = LocalSpread(me, 1, sec, lsems)
    local.start()
    butterfly(2, 3)
    for z, x in zip(zs, xs[1:]):
        z.add()
        x.start(0)
        x.start(1)
    local.finish()
    butterfly(3, 99)
    for c in zs + xs:
        c.finish()


def pick(v, index, dim):
    return lax.dynamic_index_in_dim(v, index, dim, keepdims=False)


def shards(x_in, cotangent, layout, w_qkv, b_qv, w_out, w_fc1, b_fc1, w_fc2, gains, biases):
    s, zl, t = (lax.axis_index(a) for a in ("s", "zl", "t"))
    outer = lax.axis_size("zh")
    far, nb = outer * 2, outer * 4
    log_outer = outer.bit_length() - 1
    mb, rows_mb, width = x_in.shape
    wrows = w_out.shape[1]
    block = w_out.shape[2]
    hid = w_fc1.shape[2]
    cq, hq = block // 4, hid // 4
    share = rows_mb // 4
    tokens = (2, mb, 2, 2, share, width)

    quarter = s * 2 + zl
    own_vecs = jnp.concatenate([jnp.stack([gains[0, 0], biases[0, 0], gains[0, 1], biases[0, 1]]), biases[0, 2:]])
    own_pen = jax.vmap(geometry)(layout.reshape(mb, rows_mb)).astype(BF)
    local_heads = cq // HEAD_DIM
    head_ids = t * (block // HEAD_DIM) + quarter * local_heads + jnp.arange(local_heads, dtype=jnp.int32)
    slopes = jnp.exp2(-8.0 * (head_ids + 1).astype(F32) / HEADS)

    own_shape = (mb, 2, 2, share, width)
    qk, oo, ff = (3, cq), (1, cq), (1, hq)
    att_w = [((3, nb, wrows, cq), BF), ((1, nb, wrows, cq), BF)]
    ff_w = [((1, nb, wrows, hq), BF)] * 2
    own_rows = (mb, share, width)
    hidden_shape = (2, mb, rows_mb, hq)
    proj_shape = (3, 2, mb, rows_mb, cq)
    mixed_shape = (2, mb, rows_mb, cq)
    act_scratch = sums_scratch(mb, share, width)
    halves = [((2, k, wrows, 2 * c), BF) for k, c in (qk, oo, ff, ff)]
    stash_outs = [
        (tokens, BF),
        (proj_shape, BF),
        (mixed_shape, BF),
        (own_rows, BF),
        (own_rows, F32),
        (tokens, BF),
    ]
    outs = [(tokens, BF), (own_shape, BF)]
    outs += [((2, 6, width), F32), ((2, 1, hq), F32), ((2, mb, GROUP, GROUP), BF)]
    outs += halves + (att_w + ff_w) * 2 + stash_outs * 2
    sem = pltpu.SemaphoreType.DMA
    cot, x1, vecs, bias_up, pen, _, _, _, _, wqkv0, wo0, wup0, wdn0, wqkv1, wo1, wup1, wdn1, *stashed = call(
        forward_all,
        0,
        (
            w_qkv[0].transpose(1, 0, 2),
            w_out,
            w_fc1,
            w_fc2,
            x_in.reshape(own_shape),
            cotangent.reshape(own_shape),
            b_qv[0],
            b_fc1,
            own_vecs,
            slopes,
            own_pen,
        ),
        [AN] * 6 + [VM] * 3 + [SM, VM],
        outs,
        [AN] * 2 + [VM] * 3 + [AN] * (len(outs) - 5),
        act_scratch
        + [sem((8, 4))] * 2
        + [pltpu.VMEM(tokens, BF)] * 3
        + [pltpu.VMEM(sh, BF) for sh in (proj_shape, mixed_shape, hidden_shape)]
        + [pltpu.VMEM(own_rows, F32), pltpu.VMEM(own_rows, BF)]
        + [pltpu.VMEM(sh, dt) for sh, dt in att_w + ff_w]
        + [sem((6,)), sem((13,)), sem((4, 4)), sem((2, 6)), pltpu.VMEM(own_shape, BF)]
        + [sem((2, 4)), pltpu.VMEM((2, 2, block), F32), pltpu.VMEM((2, 1, hid), F32)]
        + [pltpu.VMEM((k, wrows, 2 * c), BF) for k, c in (qk, oo, ff, ff)]
        + fetch_scratch((qk, oo), far, wrows)
        + fetch_scratch((ff, ff), far, wrows)
        + [sem((2, 5, far))] * 2,
    )
    normed0, proj0, mixed0, xo0, hidden0, nt0, normed1, proj1, mixed1, xo1, hidden1, nt1 = stashed
    wup0, wdn0, wup1, wdn1 = (w.reshape(width, hq) for w in (wup0, wdn0, wup1, wdn1))

    def ff_bwd(layer, cid, ins, plan, arrays):
        m_specs, m_outs, m_out_specs, m_scratch = moves_parts(plan, bool(plan[0]), far, wrows)
        outs = [
            ((1, nb, wrows, hq), BF),
            ((1, nb, wrows, hq), BF),
            (hidden_shape, BF),
            (own_rows, F32),
            ((4, 8, width), F32),
            ((8, hq), F32),
            (tokens, BF),
            ((1, far - 1, wrows, hq), BF),
        ]
        scratch = act_scratch + [
            pltpu.VMEM(hidden_shape, BF),
            pltpu.SemaphoreType.DMA((3, far)),
            pltpu.VMEM((1, nb, wrows, hq), BF),
            pltpu.VMEM((1, nb, wrows, hq), BF),
            pltpu.VMEM(hidden_shape, BF),
            sem((3,)),
            pltpu.VMEM(tokens, BF),
            pltpu.VMEM(tokens, BF),
            pltpu.VMEM((width, hq), BF),
            pltpu.VMEM((width, hq), BF),
            sem((4,)),
        ]
        return call(
            functools.partial(ff_backward, layer, tuple(len(p) for p in plan)),
            cid,
            list(ins) + list(arrays),
            [AN] * 4 + [VM] * (len(ins) - 4) + m_specs,
            outs + m_outs,
            [AN] * 3 + [VM] * (len(outs) - 3) + m_out_specs,
            scratch + m_scratch,
        )

    def att_bwd(layer, cid, ins, plan, arrays):
        last = layer == 0
        m_specs, m_outs, m_out_specs, m_scratch = moves_parts(plan, last, far, wrows)
        outs = att_w + [((2, 8, width), F32), ((3, 8, cq), F32), (own_shape if last else tokens, BF)]
        scratch = act_scratch + [pltpu.VMEM(proj_shape, BF), sem((2, 3)), sem((2, 2)), sem((2, 3, far))]
        scratch += [pltpu.VMEM(sh, dt) for sh, dt in [(tokens, BF), (mixed_shape, BF)] + att_w] + [sem((4,))]
        return call(
            functools.partial(att_backward, layer, last, tuple(len(p) for p in plan)),
            cid,
            list(ins) + list(arrays),
            [VM, VM, AN, VM, AN] + [VM] * 3 + [SM, VM, VM] + m_specs,
            outs + m_outs + ([((1, wrows, 2 * hq), BF)] + [((k, far - 1, wrows, c), BF) for k, c in (qk, oo)]) * last,
            [AN, AN] + [VM] * (len(outs) - 2) + m_out_specs + [AN, VM, VM] * last,
            scratch + m_scratch,
        )

    wqkv0, wo0 = wqkv0.reshape(3, width, cq), wo0.reshape(width, cq)
    wqkv1, wo1 = wqkv1.reshape(3, width, cq), wo1.reshape(width, cq)
    g_up1, g_dn1, act1, gh1, sf1, su1, gb1, dn1_total = ff_bwd(
        1, 4, (cot, nt1, wup1, wdn1, vecs, hidden1, bias_up), ((), (), ()), ()
    )
    g_qkv1, g_o1, sa1, sp1, g0, up1_total, h_dn1 = att_bwd(
        1,
        5,
        (gb1, xo1, normed1, proj1, mixed1, wqkv1, wo1, vecs, slopes, pen, gh1),
        ((ff,), (ff,), ()),
        (g_up1, dn1_total, g_dn1),
    )
    g_up0, g_dn0, _, gh0, sf0, su0, gb0, dn0_total, _, _, h_up1, x_dn1, h_qkv1, h_o1 = ff_bwd(
        0,
        6,
        (g0, nt0, wup0, wdn0, vecs, hidden0, bias_up),
        ((qk, oo), (ff,), (ff,)),
        (g_qkv1, g_o1, up1_total, g_up1, h_dn1),
    )
    g_qkv0, g_o0, sa0, sp0, gin, _, h_dn0, x_up1, x_qkv1, x_o1, h_up0, x_dn0, qkv0_total, o0_total = att_bwd(
        0,
        7,
        (gb0, xo0, normed0, proj0, mixed0, wqkv0, wo0, vecs, slopes, pen, gh0),
        ((ff,), (ff,), (ff, qk, oo)),
        (g_up0, dn0_total, g_dn0, h_up1, h_qkv1, h_o1),
    )

    n_small = 2 * (6 + (16 * cq + 8 * hq) // width)

    def half(k, c):
        return ((k, wrows, 2 * c), BF)

    x_up0, h_qkv0, h_o0, x_qkv0, x_o0, sec1, total = call(
        functools.partial(last_sums, log_outer),
        8,
        (act1, wdn1, hidden1, vecs, sf0, su0, sa0, sp0, sf1, su1, sa1, sp1)
        + (qkv0_total, o0_total, g_qkv0, g_o0, h_up0),
        [AN] * 2 + [VM] * 12 + [AN] * 3,
        [half(*ff), half(*qk), half(*oo), half(*qk), half(*oo)] + [(own_shape, BF), ((n_small, width), F32)],
        [AN] + [VM] * 2 + [AN] * 2 + [VM] * 2,
        act_scratch
        + [sem((2, 3)), sem((3, 2, 2)), pltpu.VMEM((4 + log_outer, n_small, width), F32), sem((2, 4 + log_outer))]
        + [pltpu.VMEM(hidden_shape, BF), pltpu.VMEM((width, hq), BF), sem((2,))]
        + z_scratch(*qk, far, wrows)
        + z_scratch(*oo, far, wrows),
    )

    def home(own0, got0, own1, got1):
        left = jnp.where(s == 0, own0, got1)
        right = jnp.where(s == 0, got0, own1)
        return jnp.concatenate([left, right], axis=-1).astype(F32)

    g_qkv = home(h_qkv0, x_qkv0, h_qkv1, x_qkv1).transpose(1, 0, 2)[None]
    g_out = home(h_o0, x_o0, h_o1, x_o1)
    g_fc1 = home(h_up0, x_up0, h_up1, x_up1)
    g_fc2 = home(h_dn0, x_dn0, h_dn1, x_dn1)

    def of_layer(first, second):
        return jnp.where(s == 0, first.reshape(mb, rows_mb, width), second.reshape(mb, rows_mb, width))[None]

    section_outputs = of_layer(x1, sec1)
    input_grads = of_layer(gin, pick(g0, zl, 0))
    total = pick(total.reshape(2, n_small // 2, width), s, 0)
    n_qv = 16 * cq // width
    grad_gains = total[:2][None]
    grad_biases = total[2:6][None]
    grad_b_qv = pick(total[6 : 6 + n_qv].reshape(1, 2, 2, 4 * cq), t, 2)
    grad_b_fc1 = pick(total[6 + n_qv :].reshape(1, 2, 4 * hq), t, 1)
    return section_outputs, input_grads, g_qkv, grad_b_qv, g_out, g_fc1, grad_b_fc1, g_fc2, grad_gains, grad_biases


def solution(mesh):
    n_s, n_dp, n_t = mesh.shape["section"], mesh.shape["dp"], mesh.shape["tensor"]
    fine = Mesh(mesh.devices.reshape(n_s, n_dp // 4, 2, 2, n_t), ("s", "zh", "zl", "y", "t"))
    return jax.shard_map(
        shards,
        mesh=fine,
        in_specs=(
            P(None, DP, None),
            P(None, DP, None),
            P(None, DP),
            P("s", DP, None, "t"),
            P("s", None, "t"),
            P("s", DP, "t"),
            P("s", DP, "t"),
            P("s", "t"),
            P("s", DP, "t"),
            P("s", None, None),
            P("s", None, None),
        ),
        out_specs=(
            P("s", None, DP, None),
            P("s", None, DP, None),
            P("s", DP, None, "t"),
            P("s", None, "t"),
            P("s", DP, "t"),
            P("s", DP, "t"),
            P("s", "t"),
            P("s", DP, "t"),
            P("s", None, None),
            P("s", None, None),
        ),
        check_vma=False,
    )
```
